512 devices in a mesh: lat: 16 (over y_hi, z), lon: 32 (over x, y_lo, core).
Axes of the slice: x: 4, y: 8 (y_hi: 2, y_lo: 4; y = y_hi * 4 + y_lo), z: 8, core: 2. Of those that a mesh axis runs over, the one named last changes fastest.
Arguments:
- fields: bfloat16 [128, 1024, 256], P('lat', 'lon'), may hold values from -6 to 6
- kernel: bfloat16 [3, 3, 256, 256], replicated, may hold values from -0.125 to 0.125
- bias: float32 [256], replicated, may hold values from -3 to 3
- target: bfloat16 [128, 1024, 256], P('lat', 'lon'), may hold values from -12 to 12
- tile_list: int32 [1024], replicated, may hold values from 0 to 1023, each once
- tail_count: int32 [32], replicated, may hold values from 384 to 768
- region_weight: float32 [32], replicated, may hold values from 2000 to 20000
Outputs:
- grad_fields: bfloat16 [128, 1024, 256], P('lat', 'lon')
- grad_kernel: bfloat16 [3, 3, 256, 256], replicated
- grad_bias: float32 [256], replicated
- region_loss: float32 [32], replicated
The draws below stay inside these ranges and needn't reach their ends.
Inputs may be any that keep to these rules, and one draw needn't show every extreme that they name: `tile_list`: each tile number appears once, so the regions split the grid into 32 parts of 32 tiles each.
All inputs are finite; a program needn't handle non-finite values.
Results may differ from the reference program's by a relative error of at most 0.0049.
Values may be sent and summed in bfloat16 or wider, within the bound.
A program may use at most 64 MiB of HBM per device.

```python
import math
import jax
import jax.numpy as jnp

C = 256
NREG = 32
ITERS = 6
NLAT = 128
NLON = 1024
NTILES = 1024
TILES_REG = 32


def draw_target(key, part):
    key_tile = jax.random.fold_in(key, 11)
    key_point = jax.random.fold_in(key, 12)
    key_noise = jax.random.fold_in(key, 13)
    tile_amp = jnp.exp(jax.random.uniform(key_tile, (NLAT // 8, NLON // 16), jnp.float32, math.log(0.8), math.log(1.25)))
    point_amp = jnp.exp(jax.random.uniform(key_point, (NLAT, NLON), jnp.float32, math.log(0.45), math.log(2.2)))
    noise = jnp.clip(jax.random.normal(key_noise, (NLAT, NLON, C), jnp.float32), -2.5, 2.5)
    spread_tiles = jnp.repeat(jnp.repeat(tile_amp, 8, axis=0), 16, axis=1)
    amplitude = spread_tiles * point_amp
    return (amplitude[:, :, None] * noise).astype(jnp.bfloat16)


def with_ends(array, stream_key, low, largest):
    shape = array.shape
    spot = [jax.random.randint(jax.random.fold_in(stream_key, axis), (), 0, shape[axis]) for axis in range(len(shape))]
    array = array.at[tuple(spot)].set(low)
    longest = shape.index(max(shape))
    spot[longest] = (spot[longest] + 1) % shape[longest]
    return array.at[tuple(spot)].set(largest)


def levels(rng, dims, split, low, largest):
    def one(dim, shards_of):
        draws = jax.random.uniform(jax.random.fold_in(jax.random.fold_in(rng, 6), dim), (shards_of,), jnp.float32, low / len(split), largest / len(split))
        return jnp.repeat(jnp.exp(draws), dims[dim] // shards_of).reshape((-1,) + (1,) * (len(dims) - dim - 1))

    gain = one(*split[0])
    for cut in split[1:]:
        gain = gain * one(*cut)
    return gain


def gaussian(key, extent, width, most, split=(), kind=jnp.bfloat16):
    gain = levels(key, extent, split, -0.22, 0.18) if split else 1.0
    entries = jax.random.normal(key, extent, jnp.float32) * width * gain
    return jnp.minimum(jnp.maximum(entries, -most), most).astype(kind)


def setup_inputs(seed: int = 0) -> dict:
    key_list = jax.random.split(jax.random.key(seed), 8)
    fields = gaussian(key_list[0], (NLAT, NLON, C), 1.0, 6.0, ((0, 16), (1, 32)))
    kernel = gaussian(key_list[1], (3, 3, C, C), (9 * C) ** -0.5, 0.125)
    bias = gaussian(key_list[2], (C,), 0.5, 3.0, (), jnp.float32)
    target = draw_target(jax.random.fold_in(key_list[7], 71), 0)
    tile_list = jax.random.permutation(key_list[4], NTILES).astype(jnp.int32)
    tail_count = with_ends(jax.random.randint(key_list[5], (NREG,), TILES_REG * 12, TILES_REG * 24 + 1), jax.random.fold_in(key_list[5], 1), TILES_REG * 12, TILES_REG * 24).astype(jnp.int32)
    region_weight = jnp.clip(jnp.exp(jax.random.uniform(key_list[6], (NREG,), jnp.float32, math.log(2000.0), math.log(20000.0))), 2000.0, 20000.0)
    return dict(fields=fields, kernel=kernel, bias=bias, target=target, tile_list=tile_list, tail_count=tail_count, region_weight=region_weight)


SMOOTH = 0.05
STEP_LIMIT = 0.3
DAMPING = 0.4
GELU_SCALE = 0.7978845608
GELU_CUBIC = 0.044715


def gelu_pair(value):
    inner = GELU_SCALE * (value + GELU_CUBIC * value * value * value)
    tangent = jnp.tanh(inner)
    act = 0.5 * value * (1.0 + tangent)
    slope = 0.5 * (1.0 + tangent) + 0.5 * value * (1.0 - tangent * tangent) * GELU_SCALE * (1.0 + 3.0 * GELU_CUBIC * value * value)
    return act, slope


def extend(field):
    wrapped = jnp.concatenate([field[:, -1:], field, field[:, :1]], axis=1)
    return jnp.pad(wrapped, ((1, 1), (0, 0), (0, 0)))


def reference(fields, kernel, bias, target, tile_list, tail_count, region_weight):
    nlat, nlon, chans = fields.shape
    count_pts = nlat * nlon
    padded = extend(fields)
    pre = jnp.zeros((count_pts, chans), jnp.float32)
    for a in range(3):
        for b in range(3):
            patch = padded[a:a + nlat, b:b + nlon].reshape(count_pts, chans)
            pre = pre + jnp.dot(patch, kernel[a, b], preferred_element_type=jnp.float32)
    pre = pre + bias
    act, slope = gelu_pair(pre)
    diff = act - target.reshape(count_pts, chans).astype(jnp.float32)
    rows = jnp.arange(nlat).astype(jnp.float32)
    lat_w = jnp.cos(jnp.pi * (rows + 0.5) / nlat - jnp.pi / 2)
    err = lat_w[:, None] * jnp.mean(diff * diff, axis=1).reshape(nlat, nlon)
    tile_rows = nlat // 8
    tile_cols = nlon // 16
    ntiles = tile_rows * tile_cols
    per_region = ntiles // NREG
    region_of = jnp.zeros((ntiles,), jnp.int32).at[tile_list].set((jnp.arange(ntiles) // per_region).astype(jnp.int32))
    count = tail_count.astype(jnp.float32)

    def per_tile(values):
        tiles = values.reshape(tile_rows, 8, tile_cols, 16).sum(axis=(1, 3)).reshape(-1)
        return jax.ops.segment_sum(tiles, region_of, NREG)

    def to_points(region_values):
        tiles = region_values[region_of].reshape(tile_rows, 1, tile_cols, 1)
        return jnp.broadcast_to(tiles, (tile_rows, 8, tile_cols, 16)).reshape(nlat, nlon)

    thresh = 2.0 * per_tile(err) / float(per_region * 128)
    for step in range(ITERS):
        sig = jax.nn.sigmoid((err - to_points(thresh)) / SMOOTH)
        above = per_tile(sig)
        spread = per_tile(sig * (1.0 - sig))
        thresh = thresh + jnp.clip(DAMPING * SMOOTH * (above - count) / (spread + 1.0), -STEP_LIMIT, STEP_LIMIT)
    scaled = (err - to_points(thresh)) / SMOOTH
    sig = jax.nn.sigmoid(scaled)
    soft_total = per_tile(SMOOTH * jax.nn.softplus(scaled))
    region_loss = thresh + soft_total / count
    d_err = to_points(region_weight / count) * sig * lat_w[:, None]
    grad_pre = (d_err.reshape(count_pts, 1) * (2.0 / chans) * diff * slope).astype(jnp.bfloat16)
    gpad = extend(grad_pre.reshape(nlat, nlon, chans))
    grad_fields = jnp.zeros((count_pts, chans), jnp.float32)
    rows_list = []
    for a in range(3):
        cols_list = []
        for b in range(3):
            patch = gpad[2 - a:2 - a + nlat, 2 - b:2 - b + nlon].reshape(count_pts, chans)
            grad_fields = grad_fields + jnp.dot(patch, kernel[a, b].T, preferred_element_type=jnp.float32)
            source = padded[a:a + nlat, b:b + nlon].reshape(count_pts, chans)
            cols_list.append(jnp.dot(source.T, grad_pre, preferred_element_type=jnp.float32))
        rows_list.append(jnp.stack(cols_list))
    grad_kernel = jnp.stack(rows_list).astype(jnp.bfloat16)
    grad_bias = jnp.sum(grad_pre.astype(jnp.float32), axis=0)
    grad_fields = grad_fields.reshape(nlat, nlon, chans).astype(jnp.bfloat16)
    return grad_fields, grad_kernel, grad_bias, region_loss
```

```python
import functools

import jax
import jax.numpy as jnp
import numpy as np
from jax import lax
from jax.experimental import pallas as pl
from jax.experimental.pallas import tpu as pltpu
from jax.sharding import PartitionSpec as P

NREG = 32
ITERS = 6
SMOOTH = 0.05
STEP_LIMIT = 0.3
DAMPING = 0.4
GELU_SCALE = 0.7978845608
GELU_CUBIC = 0.044715

MESH = pl.DeviceIdType.MESH
NLAT, NLON = 16, 32
NX, NY, NZ = 4, 8, 8
ROWS, COLS, C = 8, 32, 256
NPTS = ROWS * COLS
F32, BF16 = jnp.float32, jnp.bfloat16


def gelu_pair(value):
    inner = GELU_SCALE * (value + GELU_CUBIC * value * value * value)
    tangent = jnp.tanh(inner)
    act = 0.5 * value * (1.0 + tangent)
    slope = 0.5 * (1.0 + tangent) + 0.5 * value * (1.0 - tangent * tangent) * GELU_SCALE * (
        1.0 + 3.0 * GELU_CUBIC * value * value
    )
    return act, slope


def position():
    lat, lon = lax.axis_index("lat"), lax.axis_index("lon")
    x, y, z, core = lon // 8, (lat // 8) * 4 + (lon % 8) // 2, lat % 8, lon % 2
    return lat, lon, x, y, z, core


def device_at(x, y, z, core):
    return ((y // 4) * 8 + z, x * 8 + (y % 4) * 2 + core)


def halo_peers(lat, lon):
    steps = ((0, -1), (0, 1), (-1, 0), (1, 0), (-1, -1), (-1, 1), (1, -1), (1, 1))
    return [((lat + dl + NLAT) % NLAT, (lon + dn + NLON) % NLON) for dl, dn in steps]


def line_peers(x, y, z, core):
    zs = [device_at(x, y, (z + k) % NZ, core) for k in range(1, NZ)]
    ys = [device_at(x, (y + k) % NY, z, core) for k in range(1, NY)]
    xs = [device_at((x + k) % NX, y, z, core) for k in range(1, NX)]
    return zs, ys, xs, [device_at(x, y, z, 1 - core)]


def body(fields, w, bias, target, small, lw,
         gf_out, gk_out, gb_out, rl_out,
         pad, shifted, colbuf, rowbuf, colrec, rowrec, ds_ref, r1, r4, pt, es,
         hsend, hrecv, gsend, grecv, zsend, zrecv):
    lat, lon, x, y, z, core = position()
    zs, ys, xs, cs = line_peers(x, y, z, core)
    halos = halo_peers(lat, lon)

    barrier = pltpu.get_barrier_semaphore()
    everyone = halos + zs + ys + xs + cs
    for peer in everyone:
        pl.semaphore_signal(barrier, inc=1, device_id=peer, device_id_type=MESH)

    def remote(src, dst, send, recv, peer):
        return pltpu.make_async_remote_copy(
            src_ref=src, dst_ref=dst, send_sem=send, recv_sem=recv,
            device_id=peer, device_id_type=MESH,
        )

    def pack(n):
        for i in range(ROWS):
            colbuf[n, 0, i : i + 1, :] = pad[1 + i, 8:9, :]
            colbuf[n, 1, i : i + 1, :] = pad[1 + i, 7 + COLS : 8 + COLS, :]

    def halo_copies(n):
        west, east = colbuf.at[n, 0], colbuf.at[n, 1]
        north, south = rowbuf.at[n, 0], rowbuf.at[n, 1]
        sources = (west, east, north, south, west, east, west, east)
        targets = (
            colrec.at[n, 0], colrec.at[n, 1], rowrec.at[n, 0], rowrec.at[n, 1],
            colrec.at[n, 2], colrec.at[n, 3], colrec.at[n, 4], colrec.at[n, 5],
        )
        return [
            remote(sources[d], targets[d], hsend.at[n, d], hrecv.at[n, d], halos[d])
            for d in range(8)
        ]

    below = (lat < NLAT - 1).astype(F32)
    above_me = (lat > 0).astype(F32)

    def place(n):
        for i in range(ROWS):
            pad[1 + i, 8 + COLS : 9 + COLS, :] = colrec[n, 0, i : i + 1, :]
            pad[1 + i, 7:8, :] = colrec[n, 1, i : i + 1, :]
        last, end = ROWS + 1, 8 + COLS
        pad[last, 8:end, :] = rowrec[n, 0].astype(F32) * below
        pad[0, 8:end, :] = rowrec[n, 1].astype(F32) * above_me
        pad[last, end : end + 1, :] = colrec[n, 2, 0:1, :] * below
        pad[last, 7:8, :] = colrec[n, 3, 0:1, :] * below
        pad[0, end : end + 1, :] = colrec[n, 4, ROWS - 1 : ROWS, :] * above_me
        pad[0, 7:8, :] = colrec[n, 5, ROWS - 1 : ROWS, :] * above_me
        for b in range(3):
            for t in range(2):
                at = 7 + b + 16 * t
                shifted[b, t] = pad[:, at : at + 16, :].astype(BF16)

    def patch(a, b):
        parts = [shifted[b, t, a : a + ROWS].reshape(NPTS // 2, C) for t in range(2)]
        return jnp.concatenate(parts, axis=0)

    for r in range(ROWS):
        pad[1 + r, 8 : 8 + COLS, :] = fields[r].astype(F32)
    pack(0)
    rowbuf[0, 0] = fields[0]
    rowbuf[0, 1] = fields[ROWS - 1]
    pl.semaphore_wait(barrier, len(everyone))
    halo = halo_copies(0)
    for copy in halo:
        copy.start()

    slot = lax.broadcasted_iota(jnp.int32, (1024, 128), 0)
    st, sz, sy = slot & 1, (slot >> 1) & 7, (slot >> 4) & 7
    sx, sc = (slot >> 7) & 3, slot >> 9
    tile = ((sy >> 2) * 8 + sz) * 64 + (sx * 8 + (sy & 3) * 2 + sc) * 2 + st
    tile = tile.astype(F32)
    for blk in range(8):
        pt[:, 128 * blk : 128 * (blk + 1)] = jnp.where(
            tile == small[blk : blk + 1, :], 1.0, 0.0
        ).astype(BF16)

    for copy in halo:
        copy.wait()
    place(0)

    pre = jnp.zeros((NPTS, C), F32)
    for a in range(3):
        for b in range(3):
            k = 3 * a + b
            pre = pre + jnp.dot(
                patch(a, b), w[k * C : (k + 1) * C, :], preferred_element_type=F32
            )
    pre = pre + bias[...]
    act, slope = gelu_pair(pre)
    aim = jnp.concatenate(
        [target[:, 16 * t : 16 * (t + 1), :].reshape(NPTS // 2, C) for t in range(2)], axis=0
    )
    diff = act - aim.astype(F32)
    ds_ref[...] = diff * slope
    square = diff * diff
    prow = (lax.broadcasted_iota(jnp.int32, (1, NPTS), 1) >> 4) & 7
    pcol = (lax.broadcasted_iota(jnp.int32, (NPTS, 1), 0) >> 4) & 7
    lw_row, lw_col = jnp.zeros((1, NPTS), F32), jnp.zeros((NPTS, 1), F32)
    for i in range(ROWS):
        weight = lw[lat * ROWS + i]
        lw_row = jnp.where(prow == i, weight, lw_row)
        lw_col = jnp.where(pcol == i, weight, lw_col)
    err_row = lax.dot_general(
        jnp.ones((8, C), F32), square, (((1,), (1,)), ((), ())),
        precision=lax.Precision.HIGHEST, preferred_element_type=F32,
    )[0:1, :] * (1.0 / C) * lw_row
    r1[z, 0:1, :] = err_row[:, :128]
    r1[z, 1:2, :] = err_row[:, 128:]

    def exchange(ref, slot_id, peers, first):
        copies = [
            remote(ref.at[slot_id], ref.at[slot_id], gsend.at[first + k], grecv.at[first + k], peer)
            for k, peer in enumerate(peers)
        ]
        for copy in copies:
            copy.start()
        return copies

    copies = exchange(r1, z, zs, 0)
    err_col = jnp.sum(square, axis=1, keepdims=True) * (1.0 / C) * lw_col
    for copy in copies:
        copy.wait()
    for zz in range(NZ):
        r4[core, x, y, 2 * zz : 2 * zz + 2, :] = r1[zz, 0:2, :]
    for copy in exchange(r4.at[core, x], y, ys, 7):
        copy.wait()
    for copy in exchange(r4.at[core], x, xs, 14):
        copy.wait()
    for copy in exchange(r4, core, cs, 17):
        copy.wait()

    values = jnp.transpose(r4[...].reshape(1024, 128))
    high = values.astype(BF16)
    rest = values - high.astype(F32)
    mid = rest.astype(BF16)
    low = (rest - mid.astype(F32)).astype(BF16)
    three = jnp.concatenate([high, mid, low], axis=0)
    for blk in range(4):
        part = jnp.dot(three, pt[:, 256 * blk : 256 * (blk + 1)], preferred_element_type=F32)
        es[:, 256 * blk : 256 * (blk + 1)] = part[:128] + part[128:256] + part[256:]

    def fold(value):
        total = value[:, 0:128]
        for blk in range(1, 8):
            total = total + value[:, 128 * blk : 128 * (blk + 1)]
        total = jnp.sum(total, axis=0, keepdims=True)
        total = jnp.broadcast_to(total, (8, 128))
        total = total + pltpu.roll(total, 64, 1)
        return total + pltpu.roll(total, 32, 1)

    points = float(NPTS // 2 * 32)
    count = jnp.broadcast_to(small[8:9, :], (8, 128))
    weight = jnp.broadcast_to(small[9:10, :], (8, 128))

    def lanes(thresh):
        return jnp.concatenate([thresh[0:1, :]] * 8, axis=1)

    thresh = 2.0 * fold(es[...]) / points

    def iterate(_, thresh):
        half = (es[...] - lanes(thresh)) * (0.5 / SMOOTH)
        tangent = jnp.tanh(half)
        above = 0.5 * (fold(tangent) + points)
        spread = 0.25 * fold(1.0 - tangent * tangent)
        return thresh + jnp.clip(
            DAMPING * SMOOTH * (above - count) / (spread + 1.0), -STEP_LIMIT, STEP_LIMIT
        )

    thresh = lax.fori_loop(0, ITERS, iterate, thresh)

    numbers = small[0:8, :]
    ratio = weight / count
    half_rows = lax.broadcasted_iota(jnp.int32, (NPTS, 1), 0) < NPTS // 2
    own_thresh, own_ratio = [], []
    for t in range(2):
        mine = numbers == (lat * 64 + lon * 2 + t).astype(F32)
        for source, sink in ((thresh, own_thresh), (ratio, own_ratio)):
            picked = jnp.where(mine, source, 0.0)
            sink.append(jnp.sum(jnp.sum(picked, axis=0, keepdims=True), axis=1, keepdims=True))
    my_thresh = jnp.where(half_rows, own_thresh[0], own_thresh[1])
    my_ratio = jnp.where(half_rows, own_ratio[0], own_ratio[1])
    sig = 1.0 / (1.0 + jnp.exp((my_thresh - err_col) * (1.0 / SMOOTH)))
    d_err = my_ratio * sig * lw_col
    gp = ((d_err * (2.0 / C)) * ds_ref[...]).astype(BF16)
    for t in range(2):
        piece = gp[t * 128 : (t + 1) * 128, :].reshape(ROWS, 16, C)
        pad[1 : 1 + ROWS, 8 + 16 * t : 24 + 16 * t, :] = piece.astype(F32)
        rowbuf[1, 0, 16 * t : 16 * (t + 1), :] = piece[0]
        rowbuf[1, 1, 16 * t : 16 * (t + 1), :] = piece[ROWS - 1]
    pack(1)
    halo = halo_copies(1)
    for copy in halo:
        copy.start()

    gb_out[...] = jnp.sum(gp.astype(F32), axis=0, keepdims=True)
    for a in range(3):
        for b in range(3):
            k = 3 * a + b
            gk_out[k * C : (k + 1) * C, :] = lax.dot_general(
                patch(a, b), gp, (((0,), (0,)), ((), ())), preferred_element_type=F32
            )

    scaled = (es[...] - lanes(thresh)) * (1.0 / SMOOTH)
    soft = jnp.maximum(scaled, 0.0) + jnp.log1p(jnp.exp(-jnp.abs(scaled)))
    rl_out[...] = (thresh + SMOOTH * fold(soft) / count)[0:1, :]

    for copy in halo:
        copy.wait()
    place(1)
    total = jnp.zeros((NPTS, C), F32)
    for a in range(3):
        for b in range(3):
            k = 3 * a + b
            total = total + lax.dot_general(
                patch(2 - a, 2 - b), w[k * C : (k + 1) * C, :],
                (((1,), (1,)), ((), ())), preferred_element_type=F32,
            )
    total = total.astype(BF16)
    for t in range(2):
        gf_out[:, 16 * t : 16 * (t + 1), :] = total[t * 128 : (t + 1) * 128].reshape(ROWS, 16, C)


def on_device(fields, kernel, bias, target, tile_list, tail_count, region_weight):
    nlat = NLAT * ROWS
    lat_w = jnp.asarray(
        np.cos(np.pi * (np.arange(nlat) + 0.5) / nlat - np.pi / 2).astype(np.float32)
    )
    order = tile_list.reshape(NREG, -1).T.reshape(8, 128).astype(F32)
    small = jnp.concatenate(
        [
            order,
            jnp.tile(tail_count.astype(F32), 4)[None],
            jnp.tile(region_weight, 4)[None],
            jnp.zeros((6, 128), F32),
        ],
        axis=0,
    )
    vmem = pl.BlockSpec(memory_space=pltpu.VMEM)
    dma = pltpu.SemaphoreType.DMA
    gf, gk, gb, rl = pl.pallas_call(
        body,
        out_shape=(
            jax.ShapeDtypeStruct((ROWS, COLS, C), BF16),
            jax.ShapeDtypeStruct((9 * C, C), F32),
            jax.ShapeDtypeStruct((1, C), F32),
            jax.ShapeDtypeStruct((1, 128), F32),
        ),
        in_specs=[vmem] * 5 + [pl.BlockSpec(memory_space=pltpu.SMEM)],
        out_specs=(vmem,) * 4,
        scratch_shapes=[
            pltpu.VMEM((ROWS + 2, 48, C), F32),
            pltpu.VMEM((3, 2, ROWS + 2, 16, C), BF16),
            pltpu.VMEM((2, 2, ROWS, C), F32),
            pltpu.VMEM((2, 2, COLS, C), BF16),
            pltpu.VMEM((2, 6, ROWS, C), F32),
            pltpu.VMEM((2, 2, COLS, C), BF16),
            pltpu.VMEM((NPTS, C), F32),
            pltpu.VMEM((NZ, 8, 128), F32),
            pltpu.VMEM((2, NX, NY, 16, 128), F32),
            pltpu.VMEM((1024, 1024), BF16),
            pltpu.VMEM((128, 1024), F32),
            dma((2, 8)), dma((2, 8)), dma((18,)), dma((18,)), dma((1,)), dma((1,)),
        ],
        compiler_params=pltpu.CompilerParams(
            collective_id=0, has_side_effects=True, vmem_limit_bytes=48 * 1024 * 1024
        ),
        name="layer",
    )(fields, kernel.reshape(9 * C, C), bias.reshape(1, C), target, small, lat_w)
    gk, gb = lax.psum((gk, gb), ("lat", "lon"))
    return gf, gk.astype(BF16).reshape(3, 3, C, C), gb.reshape(C), rl[0, :NREG]


def solution(mesh):
    placed = (P("lat", "lon", None), P(), P(), P("lat", "lon", None), P(), P(), P())
    return jax.shard_map(
        on_device,
        mesh=mesh,
        in_specs=placed,
        out_specs=(P("lat", "lon", None), P(), P(), P()),
        check_vma=False,
    )
```

```python
import functools

import jax
import jax.numpy as jnp
from jax import lax
from jax.experimental import pallas as pl
from jax.experimental.pallas import tpu as pltpu
from jax.sharding import PartitionSpec as P

NREG = 32
ITERS = 6
SMOOTH = 0.05
STEP_LIMIT = 0.3
DAMPING = 0.4
GELU_SCALE = 0.7978845608
GELU_CUBIC = 0.044715

MESH = pl.DeviceIdType.MESH
NLAT, NLON = 16, 32
NX, NY, NZ = 4, 8, 8
ROWS, COLS, C = 8, 32, 256
NPTS = ROWS * COLS
F32, BF16 = jnp.float32, jnp.bfloat16


def gelu_pair(value):
    inner = GELU_SCALE * (value + GELU_CUBIC * value * value * value)
    tangent = jnp.tanh(inner)
    act = 0.5 * value * (1.0 + tangent)
    slope = 0.5 * (1.0 + tangent) + 0.5 * value * (1.0 - tangent * tangent) * GELU_SCALE * (
        1.0 + 3.0 * GELU_CUBIC * value * value
    )
    return act, slope


def position():
    lat, lon = lax.axis_index("lat"), lax.axis_index("lon")
    x, y, z, core = lon // 8, (lat // 8) * 4 + (lon % 8) // 2, lat % 8, lon % 2
    return lat, lon, x, y, z, core


def device_at(x, y, z, core):
    return ((y // 4) * 8 + z, x * 8 + (y % 4) * 2 + core)


def halo_peers(lat, lon):
    steps = ((0, -1), (0, 1), (-1, 0), (1, 0), (-1, -1), (-1, 1), (1, -1), (1, 1))
    return [((lat + dl + NLAT) % NLAT, (lon + dn + NLON) % NLON) for dl, dn in steps]


def line_peers(x, y, z, core):
    zs = [device_at(x, y, (z + k) % NZ, core) for k in range(1, NZ)]
    ys = [device_at(x, (y + k) % NY, z, core) for k in range(1, NY)]
    xs = [device_at((x + k) % NX, y, z, core) for k in range(1, NX)]
    return zs, ys, xs, [device_at(x, y, z, 1 - core)]


def body(fields_hbm, w_hbm, bias_hbm, target_hbm, list_hbm, tail_hbm, weight_hbm,
         gf_out, gk_out, gb_out, rl_out,
         fields, w, bias, target, tiles_i, tail_i, weight_f, small, lwc,
         pad, shifted, colbuf, rowbuf, colrec, rowrec, ds_ref, r1, r4, pt, es,
         gk, cbuf, crec, hx, hy, hz, sx, sy, sz, rx, ry, rz,
         hx2, sx2, rx2, sy2, ry2, sz2, rz2, ex, ey, ez, fy, fz, gb0, gbx, gby, gbz,
         lsem, hsend, hrecv, gsend, grecv, asend, arecv):
    lat, lon, x, y, z, core = position()
    loads = [
        pltpu.make_async_copy(src, dst, lsem.at[n])
        for n, (src, dst) in enumerate((
            (fields_hbm, fields), (list_hbm, tiles_i), (tail_hbm, tail_i),
            (weight_hbm, weight_f), (w_hbm, w), (bias_hbm, bias), (target_hbm, target),
        ))
    ]
    for load in loads:
        load.start()
    zs, ys, xs, cs = line_peers(x, y, z, core)
    halos = halo_peers(lat, lon)

    barrier = pltpu.get_barrier_semaphore()
    everyone = halos + zs + ys + xs + cs
    for peer in everyone:
        pl.semaphore_signal(barrier, inc=1, device_id=peer, device_id_type=MESH)

    def remote(src, dst, send, recv, peer):
        return pltpu.make_async_remote_copy(
            src_ref=src, dst_ref=dst, send_sem=send, recv_sem=recv,
            device_id=peer, device_id_type=MESH,
        )

    def pack(n):
        for i in range(ROWS):
            colbuf[n, 0, i : i + 1, :] = pad[1 + i, 8:9, :]
            colbuf[n, 1, i : i + 1, :] = pad[1 + i, 7 + COLS : 8 + COLS, :]

    def halo_copies(n):
        west, east = colbuf.at[n, 0], colbuf.at[n, 1]
        north, south = rowbuf.at[n, 0], rowbuf.at[n, 1]
        sources = (west, east, north, south, west, east, west, east)
        targets = (
            colrec.at[n, 0], colrec.at[n, 1], rowrec.at[n, 0], rowrec.at[n, 1],
            colrec.at[n, 2], colrec.at[n, 3], colrec.at[n, 4], colrec.at[n, 5],
        )
        return [
            remote(sources[d], targets[d], hsend.at[n, d], hrecv.at[n, d], halos[d])
            for d in range(8)
        ]

    below = (lat < NLAT - 1).astype(F32)
    above_me = (lat > 0).astype(F32)

    def place(n):
        for i in range(ROWS):
            pad[1 + i, 8 + COLS : 9 + COLS, :] = colrec[n, 0, i : i + 1, :]
            pad[1 + i, 7:8, :] = colrec[n, 1, i : i + 1, :]
        last, end = ROWS + 1, 8 + COLS
        pad[last, 8:end, :] = rowrec[n, 0].astype(F32) * below
        pad[0, 8:end, :] = rowrec[n, 1].astype(F32) * above_me
        pad[last, end : end + 1, :] = colrec[n, 2, 0:1, :] * below
        pad[last, 7:8, :] = colrec[n, 3, 0:1, :] * below
        pad[0, end : end + 1, :] = colrec[n, 4, ROWS - 1 : ROWS, :] * above_me
        pad[0, 7:8, :] = colrec[n, 5, ROWS - 1 : ROWS, :] * above_me
        for b in range(3):
            for t in range(2):
                at = 7 + b + 16 * t
                shifted[b, t] = pad[:, at : at + 16, :].astype(BF16)

    def patch(a, b):
        parts = [shifted[b, t, a : a + ROWS].reshape(NPTS // 2, C) for t in range(2)]
        return jnp.concatenate(parts, axis=0)

    loads[0].wait()
    for r in range(ROWS):
        pad[1 + r, 8 : 8 + COLS, :] = fields[r].astype(F32)
    pack(0)
    rowbuf[0, 0] = fields[0]
    rowbuf[0, 1] = fields[ROWS - 1]
    pl.semaphore_wait(barrier, len(everyone))
    halo = halo_copies(0)
    for copy in halo:
        copy.start()

    for load in loads[1:4]:
        load.wait()
    lane = lax.broadcasted_iota(jnp.int32, (8, 128), 1)
    row = lax.broadcasted_iota(jnp.int32, (8, 128), 0)
    wide = jnp.concatenate([tiles_i[...].astype(F32), jnp.zeros((120, 128), F32)], axis=0)
    wide = jnp.transpose(wide)
    src_b = lax.broadcasted_iota(jnp.int32, (128, 128), 0)
    dst_r = lax.broadcasted_iota(jnp.int32, (128, 128), 1) & 31
    by_member = jnp.zeros((32, 128), F32)
    for q in range(4):
        pick = jnp.where(4 * src_b + q == dst_r, 1.0, 0.0)
        by_member = by_member + jnp.dot(
            wide[32 * q : 32 * (q + 1), :], pick,
            precision=lax.Precision.HIGHEST, preferred_element_type=F32,
        )
    quarter = lane[0:1, :] >> 5
    for blk in range(8):
        line = by_member[4 * blk : 4 * blk + 1, :]
        for j in range(1, 4):
            line = jnp.where(quarter == j, by_member[4 * blk + j : 4 * blk + j + 1, :], line)
        small[blk : blk + 1, :] = line
    small[8:16, :] = jnp.zeros((8, 128), F32)
    small[8:9, 0:NREG] = tail_i[...].astype(F32)
    small[9:10, 0:NREG] = weight_f[...]
    tails = small[8:16, :]
    tails = tails + pltpu.roll(tails, 64, 1)
    small[8:16, :] = tails + pltpu.roll(tails, 32, 1)

    def lat_weight(row_in_band):
        ids = (row_in_band + lat * ROWS).astype(F32)
        return jnp.cos(jnp.pi * (ids + 0.5) / (NLAT * ROWS) - jnp.pi / 2)

    lw8 = lat_weight(row)
    for i in range(ROWS):
        for t in range(2):
            at = 128 * t + 16 * i
            lwc[at : at + 16, :] = jnp.broadcast_to(lw8[i : i + 1, :], (16, 128))
    lw_row = lat_weight((lax.broadcasted_iota(jnp.int32, (1, NPTS), 1) >> 4) & 7)

    slot = lax.broadcasted_iota(jnp.int32, (1024, 128), 0)
    at_t, at_z, at_y = slot & 1, (slot >> 1) & 7, (slot >> 4) & 7
    at_x, at_c = (slot >> 7) & 3, slot >> 9
    tile = ((at_y >> 2) * 8 + at_z) * 64 + (at_x * 8 + (at_y & 3) * 2 + at_c) * 2 + at_t
    tile = tile.astype(F32)
    for blk in range(8):
        pt[:, 128 * blk : 128 * (blk + 1)] = jnp.where(
            tile == small[blk : blk + 1, :], 1.0, 0.0
        ).astype(BF16)

    for copy in halo:
        copy.wait()
    place(0)

    for load in loads[4:]:
        load.wait()
    pre = jnp.zeros((NPTS, C), F32)
    for a in range(3):
        for b in range(3):
            k = 3 * a + b
            pre = pre + jnp.dot(
                patch(a, b), w[k * C : (k + 1) * C, :], preferred_element_type=F32
            )
    pre = pre + bias[...]
    act, slope = gelu_pair(pre)
    aim = jnp.concatenate(
        [target[:, 16 * t : 16 * (t + 1), :].reshape(NPTS // 2, C) for t in range(2)], axis=0
    )
    diff = act - aim.astype(F32)
    ds_ref[...] = diff * slope
    square = diff * diff
    lw_col = lwc[:, 0:1]
    err_row = lax.dot_general(
        jnp.ones((8, C), F32), square, (((1,), (1,)), ((), ())),
        precision=lax.Precision.HIGHEST, preferred_element_type=F32,
    )[0:1, :] * (1.0 / C) * lw_row
    r1[z, 0:1, :] = err_row[:, :128]
    r1[z, 1:2, :] = err_row[:, 128:]

    def exchange(ref, slot_id, peers, first):
        copies = [
            remote(ref.at[slot_id], ref.at[slot_id], gsend.at[first + k], grecv.at[first + k], peer)
            for k, peer in enumerate(peers)
        ]
        for copy in copies:
            copy.start()
        return copies

    copies = exchange(r1, z, zs, 0)
    err_col = jnp.sum(square, axis=1, keepdims=True) * (1.0 / C) * lw_col
    for copy in copies:
        copy.wait()
    for zz in range(NZ):
        r4[core, x, y, 2 * zz : 2 * zz + 2, :] = r1[zz, 0:2, :]
    for copy in exchange(r4.at[core, x], y, ys, 7):
        copy.wait()
    for copy in exchange(r4.at[core], x, xs, 14):
        copy.wait()
    for copy in exchange(r4, core, cs, 17):
        copy.wait()

    values = jnp.transpose(r4[...].reshape(1024, 128))
    high = values.astype(BF16)
    rest = values - high.astype(F32)
    mid = rest.astype(BF16)
    low = (rest - mid.astype(F32)).astype(BF16)
    three = jnp.concatenate([high, mid, low], axis=0)
    for blk in range(4):
        part = jnp.dot(three, pt[:, 256 * blk : 256 * (blk + 1)], preferred_element_type=F32)
        es[:, 256 * blk : 256 * (blk + 1)] = part[:128] + part[128:256] + part[256:]

    def fold(value):
        total = value[:, 0:128]
        for blk in range(1, 8):
            total = total + value[:, 128 * blk : 128 * (blk + 1)]
        total = jnp.sum(total, axis=0, keepdims=True)
        total = jnp.broadcast_to(total, (8, 128))
        total = total + pltpu.roll(total, 64, 1)
        return total + pltpu.roll(total, 32, 1)

    points = float(NPTS // 2 * 32)
    count = jnp.broadcast_to(small[8:9, :], (8, 128))
    weight = jnp.broadcast_to(small[9:10, :], (8, 128))

    def lanes(thresh):
        return jnp.concatenate([thresh[0:1, :]] * 8, axis=1)

    thresh = 2.0 * fold(es[...]) / points

    def iterate(_, thresh):
        half = (es[...] - lanes(thresh)) * (0.5 / SMOOTH)
        tangent = jnp.tanh(half)
        above = 0.5 * (fold(tangent) + points)
        spread = 0.25 * fold(1.0 - tangent * tangent)
        return thresh + jnp.clip(
            DAMPING * SMOOTH * (above - count) / (spread + 1.0), -STEP_LIMIT, STEP_LIMIT
        )

    thresh = lax.fori_loop(0, ITERS, iterate, thresh)

    numbers = small[0:8, :]
    ratio = weight / count
    half_rows = lax.broadcasted_iota(jnp.int32, (NPTS, 1), 0) < NPTS // 2
    own_thresh, own_ratio = [], []
    for t in range(2):
        mine = numbers == (lat * 64 + lon * 2 + t).astype(F32)
        for source, sink in ((thresh, own_thresh), (ratio, own_ratio)):
            picked = jnp.where(mine, source, 0.0)
            sink.append(jnp.sum(jnp.sum(picked, axis=0, keepdims=True), axis=1, keepdims=True))
    my_thresh = jnp.where(half_rows, own_thresh[0], own_thresh[1])
    my_ratio = jnp.where(half_rows, own_ratio[0], own_ratio[1])
    sig = 1.0 / (1.0 + jnp.exp((my_thresh - err_col) * (1.0 / SMOOTH)))
    d_err = my_ratio * sig * lw_col
    gp = ((d_err * (2.0 / C)) * ds_ref[...]).astype(BF16)
    for t in range(2):
        piece = gp[t * 128 : (t + 1) * 128, :].reshape(ROWS, 16, C)
        pad[1 : 1 + ROWS, 8 + 16 * t : 24 + 16 * t, :] = piece.astype(F32)
        rowbuf[1, 0, 16 * t : 16 * (t + 1), :] = piece[0]
        rowbuf[1, 1, 16 * t : 16 * (t + 1), :] = piece[ROWS - 1]
    pack(1)
    halo = halo_copies(1)
    for copy in halo:
        copy.start()

    for a in range(3):
        for b in range(3):
            k = 3 * a + b
            tap = lax.dot_general(
                patch(a, b), gp, (((0,), (0,)), ((), ())), preferred_element_type=F32
            )
            if k == 4:
                gk[0, 1024:1152, :] = tap[0:128]
                gk[1, 0:128, :] = tap[128:256]
            elif k < 4:
                gk[0, k * C : (k + 1) * C, :] = tap
            else:
                at = k * C - 1152
                gk[1, at : at + C, :] = tap
    gb0[core] = jnp.sum(gp.astype(F32), axis=0, keepdims=True)

    used = [0]

    def send(src, dst, peer):
        n = used[0]
        used[0] += 1
        copy = remote(src, dst, asend.at[n], arecv.at[n], peer)
        copy.start()
        return copy

    def wait(copies):
        for copy in copies:
            copy.wait()

    def share(ref, slot_id, peers):
        return [send(ref.at[slot_id], ref.at[slot_id], peer) for peer in peers]

    def scatter(src, dst, me, count, peers):
        return [
            send(src.at[(me + k) % count], dst.at[k - 1], peer)
            for k, peer in zip(range(1, count), peers)
        ]

    cbuf[...] = gk[1 - core].astype(BF16)
    copies = [send(cbuf, crec, cs[0])] + share(gb0, core, cs)

    wait(halo)
    place(1)
    total = jnp.zeros((NPTS, C), F32)
    for a in range(3):
        for b in range(3):
            k = 3 * a + b
            total = total + lax.dot_general(
                patch(2 - a, 2 - b), w[k * C : (k + 1) * C, :],
                (((1,), (1,)), ((), ())), preferred_element_type=F32,
            )
    total = total.astype(BF16)
    for t in range(2):
        gf_out[:, 16 * t : 16 * (t + 1), :] = total[t * 128 : (t + 1) * 128].reshape(ROWS, 16, C)

    wait(copies)
    for parts, sends, base, size, pieces in (
        (hx, sx, 0, 128, NX), (hy, sy, 512, 48, NY), (hz, sz, 896, 32, NZ),
    ):
        for n in range(pieces):
            at = base + n * size
            chunk = gk[core, at : at + size, :] + crec[at : at + size, :].astype(F32)
            parts[n] = chunk
            sends[n] = chunk.astype(BF16)
    gbx[x] = gb0[0] + gb0[1]

    copies = (
        scatter(sx, rx, x, NX, xs) + scatter(sy, ry, y, NY, ys) + scatter(sz, rz, z, NZ, zs)
        + share(gbx, x, xs)
    )

    scaled = (es[...] - lanes(thresh)) * (1.0 / SMOOTH)
    soft = jnp.maximum(scaled, 0.0) + jnp.log1p(jnp.exp(-jnp.abs(scaled)))
    rl_out[...] = (thresh + SMOOTH * fold(soft) / count)[0:1, :]

    wait(copies)

    def gathered(own, received):
        for n in range(received.shape[0]):
            own = own + received[n].astype(F32)
        return own

    def in_order(ref):
        value = ref[0].astype(F32)
        for n in range(1, ref.shape[0]):
            value = value + ref[n].astype(F32)
        return value

    part = gathered(hx[x], rx)
    for n in range(NY):
        hx2[n] = part[16 * n : 16 * (n + 1), :]
        sx2[n] = part[16 * n : 16 * (n + 1), :].astype(BF16)
    hy[y] = gathered(hy[y], ry)
    for n in range(NZ):
        sy2[n, 0:6, :] = hy[y, 6 * n : 6 * n + 6, :]
        sy2[n, 6:8, :] = jnp.zeros((2, C), F32)
    part = gathered(hz[z], rz)
    for n in range(NX):
        sz2[n] = part[8 * n : 8 * (n + 1), :]
    gby[y] = in_order(gbx)
    wait(
        scatter(sx2, rx2, y, NY, ys) + scatter(sy2, ry2, z, NZ, zs) + scatter(sz2, rz2, x, NX, xs)
        + share(gby, y, ys)
    )

    ex[z] = gathered(hx2[y], rx2).astype(BF16)
    ey[x] = gathered(sy2[z], ry2)
    ez[y] = gathered(sz2[x], rz2)
    gbz[z] = in_order(gby)
    wait(share(ex, z, zs) + share(ey, x, xs) + share(ez, y, ys) + share(gbz, z, zs))
    gb_out[...] = in_order(gbz)

    at = pl.multiple_of(128 * x + 16 * y, 16)
    gk_out[core, pl.ds(at, 16), :] = in_order(ex).astype(BF16)
    fy[z] = in_order(ey)
    fz[x] = in_order(ez)
    mine = gk_out.at[core, pl.ds(at, 16)]
    wait([send(mine, mine, peer) for peer in ys] + share(fy, z, zs) + share(fz, x, xs))
    for n in range(NZ):
        hy[y, 6 * n : 6 * n + 6, :] = fy[n, 0:6, :]
    at_x = pl.multiple_of(128 * x, 128)
    at_y = pl.multiple_of(512 + 48 * y, 16)
    at_z = pl.multiple_of(896 + 32 * z, 16)
    gk_out[core, pl.ds(at_y, 48), :] = hy[y].astype(BF16)
    gk_out[core, pl.ds(at_z, 32), :] = fz[...].reshape(32, C).astype(BF16)
    copies = []
    for at, size, peers in ((at_x, 128, xs), (at_y, 48, ys), (at_z, 32, zs)):
        mine = gk_out.at[core, pl.ds(at, size)]
        copies += [send(mine, mine, peer) for peer in peers]
    wait(copies)
    wait(share(gk_out, core, cs))


def on_device(fields, kernel, bias, target, tile_list, tail_count, region_weight):
    vmem = pl.BlockSpec(memory_space=pltpu.VMEM)
    dma = pltpu.SemaphoreType.DMA
    v = pltpu.VMEM
    gf, gk, gb, rl = pl.pallas_call(
        body,
        out_shape=(
            jax.ShapeDtypeStruct((ROWS, COLS, C), BF16),
            jax.ShapeDtypeStruct((2, 1152, C), BF16),
            jax.ShapeDtypeStruct((1, C), F32),
            jax.ShapeDtypeStruct((1, 128), F32),
        ),
        in_specs=[pl.BlockSpec(memory_space=pl.ANY)] * 7,
        out_specs=(vmem,) * 4,
        scratch_shapes=[
            v((ROWS, COLS, C), BF16), v((9 * C, C), BF16), v((1, C), F32), v((ROWS, COLS, C), BF16),
            v((8, 128), jnp.int32), v((1, NREG), jnp.int32), v((1, NREG), F32),
            v((16, 128), F32), v((NPTS, 128), F32),
            v((ROWS + 2, 48, C), F32), v((3, 2, ROWS + 2, 16, C), BF16),
            v((2, 2, ROWS, C), F32), v((2, 2, COLS, C), BF16),
            v((2, 6, ROWS, C), F32), v((2, 2, COLS, C), BF16),
            v((NPTS, C), F32), v((NZ, 8, 128), F32), v((2, NX, NY, 16, 128), F32),
            v((1024, 1024), BF16), v((128, 1024), F32),
            v((2, 1152, C), F32), v((1152, C), BF16), v((1152, C), BF16),
            v((NX, 128, C), F32), v((NY, 48, C), F32), v((NZ, 32, C), F32),
            v((NX, 128, C), BF16), v((NY, 48, C), BF16), v((NZ, 32, C), BF16),
            v((NX - 1, 128, C), BF16), v((NY - 1, 48, C), BF16), v((NZ - 1, 32, C), BF16),
            v((NY, 16, C), F32), v((NY, 16, C), BF16), v((NY - 1, 16, C), BF16),
            v((NZ, 8, C), F32), v((NZ - 1, 8, C), F32),
            v((NX, 8, C), F32), v((NX - 1, 8, C), F32),
            v((NZ, 16, C), BF16), v((NX, 8, C), F32), v((NY, 8, C), F32),
            v((NZ, 8, C), F32), v((NX, 8, C), F32),
            v((2, 1, C), F32), v((NX, 1, C), F32), v((NY, 1, C), F32), v((NZ, 1, C), F32),
            dma((7,)), dma((2, 8)), dma((2, 8)), dma((18,)), dma((18,)), dma((105,)), dma((105,)),
        ],
        compiler_params=pltpu.CompilerParams(
            collective_id=0, has_side_effects=True, vmem_limit_bytes=60 * 1024 * 1024
        ),
        name="layer",
    )(
        fields, kernel.reshape(9 * C, C), bias.reshape(1, C), target,
        tile_list.reshape(8, 128), tail_count.reshape(1, NREG), region_weight.reshape(1, NREG),
    )
    return gf, gk.reshape(3, 3, C, C), gb.reshape(C), rl[0, :NREG]


def solution(mesh):
    placed = (P("lat", "lon", None), P(), P(), P("lat", "lon", None), P(), P(), P())
    return jax.shard_map(
        on_device,
        mesh=mesh,
        in_specs=placed,
        out_specs=(P("lat", "lon", None), P(), P(), P()),
        check_vma=False,
    )
```

```python
import functools

import jax
import jax.numpy as jnp
from jax import lax
from jax.experimental import pallas as pl
from jax.experimental.pallas import tpu as pltpu
from jax.sharding import PartitionSpec as P

NREG = 32
ITERS = 6
SMOOTH = 0.05
STEP_LIMIT = 0.3
DAMPING = 0.4
GELU_SCALE = 0.7978845608
GELU_CUBIC = 0.044715

MESH = pl.DeviceIdType.MESH
NLAT, NLON = 16, 32
NX, NY, NZ = 4, 8, 8
ROWS, COLS, C = 8, 32, 256
NPTS = ROWS * COLS
F32, BF16 = jnp.float32, jnp.bfloat16


def gelu_pair(value):
    inner = GELU_SCALE * (value + GELU_CUBIC * value * value * value)
    tangent = jnp.tanh(inner)
    act = 0.5 * value * (1.0 + tangent)
    slope = 0.5 * (1.0 + tangent) + 0.5 * value * (1.0 - tangent * tangent) * GELU_SCALE * (
        1.0 + 3.0 * GELU_CUBIC * value * value
    )
    return act, slope


def position():
    lat, lon = lax.axis_index("lat"), lax.axis_index("lon")
    x, y, z, core = lon // 8, (lat // 8) * 4 + (lon % 8) // 2, lat % 8, lon % 2
    return lat, lon, x, y, z, core


def device_at(x, y, z, core):
    return ((y // 4) * 8 + z, x * 8 + (y % 4) * 2 + core)


def halo_peers(lat, lon):
    steps = ((0, -1), (0, 1), (-1, 0), (1, 0), (-1, -1), (-1, 1), (1, -1), (1, 1))
    return [((lat + dl + NLAT) % NLAT, (lon + dn + NLON) % NLON) for dl, dn in steps]


def line_peers(x, y, z, core):
    zs = [device_at(x, y, (z + k) % NZ, core) for k in range(1, NZ)]
    ys = [device_at(x, (y + k) % NY, z, core) for k in range(1, NY)]
    xs = [device_at((x + k) % NX, y, z, core) for k in range(1, NX)]
    return zs, ys, xs, [device_at(x, y, z, 1 - core)]


def body(fields_hbm, w_hbm, bias_hbm, target_hbm, list_hbm, tail_hbm, weight_hbm,
         gf_out, gk_out, gb_out, rl_out,
         fields, w, bias, target, tiles_i, tail_i, weight_f, small, lwc,
         pad, shifted, turned, colbuf, rowbuf, colrec, rowrec, ds_ref, r1, r4, pt, es,
         gk, cbuf, crec, hx, hy, hz, sx, sy, sz, rx, ry, rz,
         hx2, sx2, rx2, sy2, ry2, sz2, rz2, ex, ey, ez, fy, fz, gb0, gbx, gby, gbz,
         lsem, hsend, hrecv, gsend, grecv, asend, arecv):
    lat, lon, x, y, z, core = position()
    loads = [
        pltpu.make_async_copy(src, dst, lsem.at[n])
        for n, (src, dst) in enumerate((
            (fields_hbm, fields), (list_hbm, tiles_i), (tail_hbm, tail_i),
            (weight_hbm, weight_f), (w_hbm, w), (bias_hbm, bias), (target_hbm, target),
        ))
    ]
    for load in loads:
        load.start()
    zs, ys, xs, cs = line_peers(x, y, z, core)
    halos = halo_peers(lat, lon)

    barrier = pltpu.get_barrier_semaphore()
    everyone = halos + zs + ys + xs + cs
    for peer in everyone:
        pl.semaphore_signal(barrier, inc=1, device_id=peer, device_id_type=MESH)

    def remote(src, dst, send, recv, peer):
        return pltpu.make_async_remote_copy(
            src_ref=src, dst_ref=dst, send_sem=send, recv_sem=recv,
            device_id=peer, device_id_type=MESH,
        )

    def pack(n):
        for i in range(ROWS):
            colbuf[n, 0, i : i + 1, :] = pad[1 + i, 8:9, :]
            colbuf[n, 1, i : i + 1, :] = pad[1 + i, 7 + COLS : 8 + COLS, :]

    def halo_copies(n):
        west, east = colbuf.at[n, 0], colbuf.at[n, 1]
        north, south = rowbuf.at[n, 0], rowbuf.at[n, 1]
        sources = (west, east, north, south, west, east, west, east)
        targets = (
            colrec.at[n, 0], colrec.at[n, 1], rowrec.at[n, 0], rowrec.at[n, 1],
            colrec.at[n, 2], colrec.at[n, 3], colrec.at[n, 4], colrec.at[n, 5],
        )
        return [
            remote(sources[d], targets[d], hsend.at[n, d], hrecv.at[n, d], halos[d])
            for d in range(8)
        ]

    below = (lat < NLAT - 1).astype(F32)
    above_me = (lat > 0).astype(F32)

    def place(n):
        for i in range(ROWS):
            pad[1 + i, 8 + COLS : 9 + COLS, :] = colrec[n, 0, i : i + 1, :]
            pad[1 + i, 7:8, :] = colrec[n, 1, i : i + 1, :]
        last, end = ROWS + 1, 8 + COLS
        pad[last, 8:end, :] = rowrec[n, 0].astype(F32) * below
        pad[0, 8:end, :] = rowrec[n, 1].astype(F32) * above_me
        pad[last, end : end + 1, :] = colrec[n, 2, 0:1, :] * below
        pad[last, 7:8, :] = colrec[n, 3, 0:1, :] * below
        pad[0, end : end + 1, :] = colrec[n, 4, ROWS - 1 : ROWS, :] * above_me
        pad[0, 7:8, :] = colrec[n, 5, ROWS - 1 : ROWS, :] * above_me
        for b in range(3):
            for t in range(2):
                at = 7 + b + 16 * t
                shifted[b, t] = pad[:, at : at + 16, :].astype(BF16)

    def patch(a, b):
        parts = [shifted[b, t, a : a + ROWS].reshape(NPTS // 2, C) for t in range(2)]
        return jnp.concatenate(parts, axis=0)

    loads[0].wait()
    for r in range(ROWS):
        pad[1 + r, 8 : 8 + COLS, :] = fields[r].astype(F32)
    pack(0)
    rowbuf[0, 0] = fields[0]
    rowbuf[0, 1] = fields[ROWS - 1]
    pl.semaphore_wait(barrier, len(everyone))
    halo = halo_copies(0)
    for copy in halo:
        copy.start()

    for load in loads[1:4]:
        load.wait()
    lane = lax.broadcasted_iota(jnp.int32, (8, 128), 1)
    row = lax.broadcasted_iota(jnp.int32, (8, 128), 0)
    wide = jnp.concatenate([tiles_i[...].astype(F32), jnp.zeros((120, 128), F32)], axis=0)
    wide = jnp.transpose(wide)
    src_b = lax.broadcasted_iota(jnp.int32, (128, 128), 0)
    dst_r = lax.broadcasted_iota(jnp.int32, (128, 128), 1) & 31
    by_member = jnp.zeros((32, 128), F32)
    for q in range(4):
        pick = jnp.where(4 * src_b + q == dst_r, 1.0, 0.0)
        by_member = by_member + jnp.dot(
            wide[32 * q : 32 * (q + 1), :], pick,
            precision=lax.Precision.HIGHEST, preferred_element_type=F32,
        )
    quarter = lane[0:1, :] >> 5
    for blk in range(8):
        line = by_member[4 * blk : 4 * blk + 1, :]
        for j in range(1, 4):
            line = jnp.where(quarter == j, by_member[4 * blk + j : 4 * blk + j + 1, :], line)
        small[blk : blk + 1, :] = line
    small[8:16, :] = jnp.zeros((8, 128), F32)
    small[8:9, 0:NREG] = tail_i[...].astype(F32)
    small[9:10, 0:NREG] = weight_f[...]
    tails = small[8:16, :]
    tails = tails + pltpu.roll(tails, 64, 1)
    small[8:16, :] = tails + pltpu.roll(tails, 32, 1)

    def lat_weight(row_in_band):
        ids = (row_in_band + lat * ROWS).astype(F32)
        return jnp.cos(jnp.pi * (ids + 0.5) / (NLAT * ROWS) - jnp.pi / 2)

    lw8 = lat_weight(row)
    for i in range(ROWS):
        for t in range(2):
            at = 128 * t + 16 * i
            lwc[at : at + 16, :] = jnp.broadcast_to(lw8[i : i + 1, :], (16, 128))
    lw_row = lat_weight((lax.broadcasted_iota(jnp.int32, (1, NPTS), 1) >> 4) & 7)

    slot = lax.broadcasted_iota(jnp.int32, (1024, 128), 0)
    at_t, at_z, at_y = slot & 1, (slot >> 1) & 7, (slot >> 4) & 7
    at_x, at_c = (slot >> 7) & 3, slot >> 9
    tile = ((at_y >> 2) * 8 + at_z) * 64 + (at_x * 8 + (at_y & 3) * 2 + at_c) * 2 + at_t
    tile = tile.astype(F32)
    for blk in range(8):
        pt[:, 128 * blk : 128 * (blk + 1)] = jnp.where(
            tile == small[blk : blk + 1, :], 1.0, 0.0
        ).astype(BF16)

    for copy in halo:
        copy.wait()
    place(0)

    for load in loads[4:]:
        load.wait()
    pre = jnp.zeros((NPTS, C), F32)
    for a in range(3):
        for b in range(3):
            k = 3 * a + b
            pre = pre + jnp.dot(
                patch(a, b), w[k * C : (k + 1) * C, :], preferred_element_type=F32
            )
    pre = pre + bias[...]
    act, slope = gelu_pair(pre)
    aim = jnp.concatenate(
        [target[:, 16 * t : 16 * (t + 1), :].reshape(NPTS // 2, C) for t in range(2)], axis=0
    )
    diff = act - aim.astype(F32)
    ds_ref[...] = diff * slope
    square = diff * diff
    lw_col = lwc[:, 0:1]
    err_row = lax.dot_general(
        jnp.ones((8, C), F32), square, (((1,), (1,)), ((), ())),
        precision=lax.Precision.HIGHEST, preferred_element_type=F32,
    )[0:1, :] * (1.0 / C) * lw_row
    r1[z, 0:1, :] = err_row[:, :128]
    r1[z, 1:2, :] = err_row[:, 128:]

    def exchange(ref, slot_id, peers, first):
        copies = [
            remote(ref.at[slot_id], ref.at[slot_id], gsend.at[first + k], grecv.at[first + k], peer)
            for k, peer in enumerate(peers)
        ]
        for copy in copies:
            copy.start()
        return copies

    def turn(taps):
        for k in taps:
            turned[k] = jnp.transpose(patch(k // 3, k % 3))

    copies = exchange(r1, z, zs, 0)
    err_col = jnp.sum(square, axis=1, keepdims=True) * (1.0 / C) * lw_col
    turn(range(4))
    for copy in copies:
        copy.wait()
    for zz in range(NZ):
        r4[core, x, y, 2 * zz : 2 * zz + 2, :] = r1[zz, 0:2, :]
    copies = exchange(r4.at[core, x], y, ys, 7)
    turn(range(4, 9))
    for copy in copies:
        copy.wait()
    copies = exchange(r4.at[core], x, xs, 14)
    passed = exchange(r4.at[core], x, cs, 17)
    for n, k in enumerate((1, 3, 2)):
        copies[k - 1].wait()
        passed += exchange(r4.at[core], (x + NX - k) % NX, cs, 18 + n)
    for copy in passed:
        copy.wait()

    values = jnp.transpose(r4[...].reshape(1024, 128))
    high = values.astype(BF16)
    rest = values - high.astype(F32)
    mid = rest.astype(BF16)
    low = (rest - mid.astype(F32)).astype(BF16)
    three = jnp.concatenate([high, mid, low], axis=0)
    for blk in range(4):
        part = jnp.dot(three, pt[:, 256 * blk : 256 * (blk + 1)], preferred_element_type=F32)
        es[:, 256 * blk : 256 * (blk + 1)] = part[:128] + part[128:256] + part[256:]

    def fold(value):
        total = value[:, 0:128]
        for blk in range(1, 8):
            total = total + value[:, 128 * blk : 128 * (blk + 1)]
        total = jnp.sum(total, axis=0, keepdims=True)
        total = jnp.broadcast_to(total, (8, 128))
        total = total + pltpu.roll(total, 64, 1)
        return total + pltpu.roll(total, 32, 1)

    points = float(NPTS // 2 * 32)
    count = jnp.broadcast_to(small[8:9, :], (8, 128))
    weight = jnp.broadcast_to(small[9:10, :], (8, 128))

    def lanes(thresh):
        return jnp.concatenate([thresh[0:1, :]] * 8, axis=1)

    thresh = 2.0 * fold(es[...]) / points

    def iterate(_, thresh):
        half = (es[...] - lanes(thresh)) * (0.5 / SMOOTH)
        tangent = jnp.tanh(half)
        above = 0.5 * (fold(tangent) + points)
        spread = 0.25 * fold(1.0 - tangent * tangent)
        return thresh + jnp.clip(
            DAMPING * SMOOTH * (above - count) / (spread + 1.0), -STEP_LIMIT, STEP_LIMIT
        )

    thresh = lax.fori_loop(0, ITERS, iterate, thresh)

    numbers = small[0:8, :]
    ratio = weight / count
    half_rows = lax.broadcasted_iota(jnp.int32, (NPTS, 1), 0) < NPTS // 2
    own_thresh, own_ratio = [], []
    for t in range(2):
        mine = numbers == (lat * 64 + lon * 2 + t).astype(F32)
        for source, sink in ((thresh, own_thresh), (ratio, own_ratio)):
            picked = jnp.where(mine, source, 0.0)
            sink.append(jnp.sum(jnp.sum(picked, axis=0, keepdims=True), axis=1, keepdims=True))
    my_thresh = jnp.where(half_rows, own_thresh[0], own_thresh[1])
    my_ratio = jnp.where(half_rows, own_ratio[0], own_ratio[1])
    sig = 1.0 / (1.0 + jnp.exp((my_thresh - err_col) * (1.0 / SMOOTH)))
    d_err = my_ratio * sig * lw_col
    gp = ((d_err * (2.0 / C)) * ds_ref[...]).astype(BF16)
    for t in range(2):
        piece = gp[t * 128 : (t + 1) * 128, :].reshape(ROWS, 16, C)
        pad[1 : 1 + ROWS, 8 + 16 * t : 24 + 16 * t, :] = piece.astype(F32)
        rowbuf[1, 0, 16 * t : 16 * (t + 1), :] = piece[0]
        rowbuf[1, 1, 16 * t : 16 * (t + 1), :] = piece[ROWS - 1]
    pack(1)
    halo = halo_copies(1)
    for copy in halo:
        copy.start()

    gb0[core] = jnp.sum(gp.astype(F32), axis=0, keepdims=True)

    def taps(which):
        for k in which:
            tap = jnp.dot(turned[k], gp, preferred_element_type=F32)
            if k == 4:
                gk[0, 1024:1152, :] = tap[0:128]
                gk[1, 0:128, :] = tap[128:256]
            elif k < 4:
                gk[0, k * C : (k + 1) * C, :] = tap
            else:
                at = k * C - 1152
                gk[1, at : at + C, :] = tap

    used = [0]

    def send(src, dst, peer):
        n = used[0]
        used[0] += 1
        copy = remote(src, dst, asend.at[n], arecv.at[n], peer)
        copy.start()
        return copy

    def wait(copies):
        for copy in copies:
            copy.wait()

    def share(ref, slot_id, peers):
        return [send(ref.at[slot_id], ref.at[slot_id], peer) for peer in peers]

    def scatter(src, dst, me, count, peers):
        return [
            send(src.at[(me + k) % count], dst.at[k - 1], peer)
            for k, peer in zip(range(1, count), peers)
        ]

    spans = {"x": (0, 512), "y": (512, 896), "z": (896, 1152)}

    def to_other_core(name):
        low, high = spans[name]
        cbuf[low:high, :] = gk[1 - core, low:high, :].astype(BF16)
        return [send(cbuf.at[low:high], crec.at[low:high], cs[0])]

    taps((2, 3, 6, 7))
    paired_y = to_other_core("y")
    taps((0, 1, 4, 5))
    paired_x = to_other_core("x")
    taps((8,))
    paired_z = to_other_core("z") + share(gb0, core, cs)

    def split(name, parts, sends, size):
        for n in range(parts.shape[0]):
            at = spans[name][0] + n * size
            chunk = gk[core, at : at + size, :] + crec[at : at + size, :].astype(F32)
            parts[n] = chunk
            sends[n] = chunk.astype(BF16)

    wait(paired_y)
    split("y", hy, sy, 48)
    first_y = scatter(sy, ry, y, NY, ys)
    wait(paired_x)
    split("x", hx, sx, 128)
    first_x = scatter(sx, rx, x, NX, xs)
    wait(paired_z)
    split("z", hz, sz, 32)
    first_z = scatter(sz, rz, z, NZ, zs)
    gbx[x] = gb0[0] + gb0[1]
    first_x += share(gbx, x, xs)

    wait(halo)
    place(1)
    total = jnp.zeros((NPTS, C), F32)
    for a in range(3):
        for b in range(3):
            k = 3 * a + b
            total = total + lax.dot_general(
                patch(2 - a, 2 - b), w[k * C : (k + 1) * C, :],
                (((1,), (1,)), ((), ())), preferred_element_type=F32,
            )
    total = total.astype(BF16)
    for t in range(2):
        gf_out[:, 16 * t : 16 * (t + 1), :] = total[t * 128 : (t + 1) * 128].reshape(ROWS, 16, C)

    scaled = (es[...] - lanes(thresh)) * (1.0 / SMOOTH)
    soft = jnp.maximum(scaled, 0.0) + jnp.log1p(jnp.exp(-jnp.abs(scaled)))
    rl_out[...] = (thresh + SMOOTH * fold(soft) / count)[0:1, 0:NREG]

    def gathered(own, received):
        for n in range(received.shape[0]):
            own = own + received[n].astype(F32)
        return own

    def in_order(ref):
        value = ref[0].astype(F32)
        for n in range(1, ref.shape[0]):
            value = value + ref[n].astype(F32)
        return value

    wait(first_x)
    part = gathered(hx[x], rx)
    for n in range(NY):
        hx2[n] = part[16 * n : 16 * (n + 1), :]
        sx2[n] = part[16 * n : 16 * (n + 1), :].astype(BF16)
    gby[y] = in_order(gbx)
    second_x = scatter(sx2, rx2, y, NY, ys) + share(gby, y, ys)

    wait(first_z)
    part = gathered(hz[z], rz)
    for n in range(NX):
        sz2[n] = part[8 * n : 8 * (n + 1), :]
    second_z = scatter(sz2, rz2, x, NX, xs)

    wait(first_y)
    hy[y] = gathered(hy[y], ry)
    for n in range(NZ):
        sy2[n, 0:6, :] = hy[y, 6 * n : 6 * n + 6, :]
        sy2[n, 6:8, :] = jnp.zeros((2, C), F32)
    second_y = scatter(sy2, ry2, z, NZ, zs)

    wait(second_x)
    ex[z] = gathered(hx2[y], rx2).astype(BF16)
    gbz[z] = in_order(gby)
    third_x = share(ex, z, zs) + share(gbz, z, zs)
    wait(second_z)
    ez[y] = gathered(sz2[x], rz2)
    third_z = share(ez, y, ys)
    wait(second_y)
    ey[x] = gathered(sy2[z], ry2)
    third_y = share(ey, x, xs)

    wait(third_x)
    at = pl.multiple_of(128 * x + 16 * y, 16)
    gk_out[core, pl.ds(at, 16), :] = in_order(ex).astype(BF16)
    mine = gk_out.at[core, pl.ds(at, 16)]
    fourth_x = [send(mine, mine, peer) for peer in ys]
    gb_out[...] = in_order(gbz)
    wait(third_y)
    fy[z] = in_order(ey)
    fourth_y = share(fy, z, zs)
    wait(third_z)
    fz[x] = in_order(ez)
    fourth_z = share(fz, x, xs)

    def spread_out(at, size, peers):
        mine = gk_out.at[core, pl.ds(at, size)]
        return [send(mine, mine, peer) for peer in peers]

    def hand_over(name):
        low, high = spans[name]
        mine = gk_out.at[core, low:high]
        return [send(mine, mine, cs[0])]

    wait(fourth_z)
    at_z = pl.multiple_of(896 + 32 * z, 16)
    gk_out[core, pl.ds(at_z, 32), :] = fz[...].reshape(32, C).astype(BF16)
    fifth_z = spread_out(at_z, 32, zs)
    wait(fourth_y)
    for n in range(NZ):
        hy[y, 6 * n : 6 * n + 6, :] = fy[n, 0:6, :]
    at_y = pl.multiple_of(512 + 48 * y, 16)
    gk_out[core, pl.ds(at_y, 48), :] = hy[y].astype(BF16)
    fifth_y = spread_out(at_y, 48, ys)
    wait(fourth_x)
    fifth_x = spread_out(pl.multiple_of(128 * x, 128), 128, xs)
    wait(fifth_z)
    last = hand_over("z")
    wait(fifth_x)
    last += hand_over("x")
    wait(fifth_y)
    last += hand_over("y")
    wait(last)


def leave(gf, gk, gb, rl, gf_out, gk_out, gb_out, rl_out, sems):
    pairs = ((gk, gk_out), (gf, gf_out), (gb, gb_out), (rl, rl_out))
    copies = [pltpu.make_async_copy(a, b, sems.at[n]) for n, (a, b) in enumerate(pairs)]
    for copy in copies:
        copy.start()
    for copy in copies:
        copy.wait()


def on_device(fields, kernel, bias, target, tile_list, tail_count, region_weight):
    vmem = pl.BlockSpec(memory_space=pltpu.VMEM)
    dma = pltpu.SemaphoreType.DMA
    v = pltpu.VMEM
    gf, gk, gb, rl = pl.pallas_call(
        body,
        out_shape=(
            jax.ShapeDtypeStruct((ROWS, COLS, C), BF16),
            jax.ShapeDtypeStruct((2, 1152, C), BF16),
            jax.ShapeDtypeStruct((1, C), F32),
            jax.ShapeDtypeStruct((1, NREG), F32),
        ),
        in_specs=[pl.BlockSpec(memory_space=pl.ANY)] * 7,
        out_specs=(vmem,) * 4,
        scratch_shapes=[
            v((ROWS, COLS, C), BF16), v((9 * C, C), BF16), v((1, C), F32), v((ROWS, COLS, C), BF16),
            v((8, 128), jnp.int32), v((1, NREG), jnp.int32), v((1, NREG), F32),
            v((16, 128), F32), v((NPTS, 128), F32),
            v((ROWS + 2, 48, C), F32), v((3, 2, ROWS + 2, 16, C), BF16), v((9, C, NPTS), BF16),
            v((2, 2, ROWS, C), F32), v((2, 2, COLS, C), BF16),
            v((2, 6, ROWS, C), F32), v((2, 2, COLS, C), BF16),
            v((NPTS, C), F32), v((NZ, 8, 128), F32), v((2, NX, NY, 16, 128), F32),
            v((1024, 1024), BF16), v((128, 1024), F32),
            v((2, 1152, C), F32), v((1152, C), BF16), v((1152, C), BF16),
            v((NX, 128, C), F32), v((NY, 48, C), F32), v((NZ, 32, C), F32),
            v((NX, 128, C), BF16), v((NY, 48, C), BF16), v((NZ, 32, C), BF16),
            v((NX - 1, 128, C), BF16), v((NY - 1, 48, C), BF16), v((NZ - 1, 32, C), BF16),
            v((NY, 16, C), F32), v((NY, 16, C), BF16), v((NY - 1, 16, C), BF16),
            v((NZ, 8, C), F32), v((NZ - 1, 8, C), F32),
            v((NX, 8, C), F32), v((NX - 1, 8, C), F32),
            v((NZ, 16, C), BF16), v((NX, 8, C), F32), v((NY, 8, C), F32),
            v((NZ, 8, C), F32), v((NX, 8, C), F32),
            v((2, 1, C), F32), v((NX, 1, C), F32), v((NY, 1, C), F32), v((NZ, 1, C), F32),
            dma((7,)), dma((2, 8)), dma((2, 8)), dma((21,)), dma((21,)), dma((110,)), dma((110,)),
        ],
        compiler_params=pltpu.CompilerParams(
            collective_id=0, has_side_effects=True, vmem_limit_bytes=60 * 1024 * 1024
        ),
        name="layer",
    )(
        fields, kernel.reshape(9 * C, C), bias.reshape(1, C), target,
        tile_list.reshape(8, 128), tail_count.reshape(1, NREG), region_weight.reshape(1, NREG),
    )
    results = (gf, gk, gb, rl)
    anywhere = pl.BlockSpec(memory_space=pl.ANY)
    gf, gk, gb, rl = pl.pallas_call(
        leave,
        out_shape=[jax.ShapeDtypeStruct(r.shape, r.dtype) for r in results],
        in_specs=[anywhere] * 4,
        out_specs=[anywhere] * 4,
        scratch_shapes=[dma((4,))],
        name="leave",
    )(*results)
    return gf, gk.reshape(3, 3, C, C), gb.reshape(C), rl.reshape(NREG)


def solution(mesh):
    placed = (P("lat", "lon", None), P(), P(), P("lat", "lon", None), P(), P(), P())
    return jax.shard_map(
        on_device,
        mesh=mesh,
        in_specs=placed,
        out_specs=(P("lat", "lon", None), P(), P(), P()),
        check_vma=False,
    )
```

```python
import functools

import jax
import jax.numpy as jnp
from jax import lax
from jax.experimental import pallas as pl
from jax.experimental.pallas import tpu as pltpu
from jax.sharding import PartitionSpec as P

NREG = 32
ITERS = 6
SMOOTH = 0.05
STEP_LIMIT = 0.3
DAMPING = 0.4
GELU_SCALE = 0.7978845608
GELU_CUBIC = 0.044715

MESH = pl.DeviceIdType.MESH
NLAT, NLON = 16, 32
NX, NY, NZ = 4, 8, 8
ROWS, COLS, C = 8, 32, 256
NPTS = ROWS * COLS
F32, BF16 = jnp.float32, jnp.bfloat16


def gelu_pair(value):
    inner = GELU_SCALE * (value + GELU_CUBIC * value * value * value)
    tangent = jnp.tanh(inner)
    act = 0.5 * value * (1.0 + tangent)
    slope = 0.5 * (1.0 + tangent) + 0.5 * value * (1.0 - tangent * tangent) * GELU_SCALE * (
        1.0 + 3.0 * GELU_CUBIC * value * value
    )
    return act, slope


def position():
    lat, lon = lax.axis_index("lat"), lax.axis_index("lon")
    x, y, z, core = lon // 8, (lat // 8) * 4 + (lon % 8) // 2, lat % 8, lon % 2
    return lat, lon, x, y, z, core


def device_at(x, y, z, core):
    return ((y // 4) * 8 + z, x * 8 + (y % 4) * 2 + core)


def halo_peers(lat, lon):
    steps = ((0, -1), (0, 1), (-1, 0), (1, 0), (-1, -1), (-1, 1), (1, -1), (1, 1))
    return [((lat + dl + NLAT) % NLAT, (lon + dn + NLON) % NLON) for dl, dn in steps]


def line_peers(x, y, z, core):
    zs = [device_at(x, y, (z + k) % NZ, core) for k in range(1, NZ)]
    ys = [device_at(x, (y + k) % NY, z, core) for k in range(1, NY)]
    xs = [device_at((x + k) % NX, y, z, core) for k in range(1, NX)]
    return zs, ys, xs, [device_at(x, y, z, 1 - core)]


def body(fields_hbm, w_hbm, bias_hbm, target_hbm, list_hbm, tail_hbm, weight_hbm,
         gf_out, gk_out, gb_out, rl_out,
         fields, w, bias, target, tiles_i, tail_i, weight_f, small, lwc,
         pad, shifted, turned, colbuf, rowbuf, colrec, rowrec, ds_ref, r1, r4, pt, es,
         gk, cbuf, crec, hx, hy, hz, sx, sy, sz, rx, ry, rz,
         hx2, sx2, rx2, sy2, ry2, sz2, rz2, ex, ey, ez, fy, fz, gb0, gbx, gby, gbz,
         lsem, hsend, hrecv, gsend, grecv, asend, arecv):
    lat, lon, x, y, z, core = position()
    loads = [
        pltpu.make_async_copy(src, dst, lsem.at[n])
        for n, (src, dst) in enumerate((
            (fields_hbm, fields), (list_hbm, tiles_i), (tail_hbm, tail_i),
            (weight_hbm, weight_f), (w_hbm, w), (bias_hbm, bias), (target_hbm, target),
        ))
    ]
    for load in loads:
        load.start()
    zs, ys, xs, cs = line_peers(x, y, z, core)
    halos = halo_peers(lat, lon)

    barrier = pltpu.get_barrier_semaphore()
    everyone = halos + zs + ys + xs + cs
    for peer in everyone:
        pl.semaphore_signal(barrier, inc=1, device_id=peer, device_id_type=MESH)

    def remote(src, dst, send, recv, peer):
        return pltpu.make_async_remote_copy(
            src_ref=src, dst_ref=dst, send_sem=send, recv_sem=recv,
            device_id=peer, device_id_type=MESH,
        )

    def pack(n):
        for i in range(ROWS):
            colbuf[n, 0, i : i + 1, :] = pad[1 + i, 8:9, :]
            colbuf[n, 1, i : i + 1, :] = pad[1 + i, 7 + COLS : 8 + COLS, :]

    def halo_copies(n):
        west, east = colbuf.at[n, 0], colbuf.at[n, 1]
        north, south = rowbuf.at[n, 0], rowbuf.at[n, 1]
        sources = (west, east, north, south, west, east, west, east)
        targets = (
            colrec.at[n, 0], colrec.at[n, 1], rowrec.at[n, 0], rowrec.at[n, 1],
            colrec.at[n, 2], colrec.at[n, 3], colrec.at[n, 4], colrec.at[n, 5],
        )
        return [
            remote(sources[d], targets[d], hsend.at[n, d], hrecv.at[n, d], halos[d])
            for d in range(8)
        ]

    below = (lat < NLAT - 1).astype(F32)
    above_me = (lat > 0).astype(F32)

    def place(n):
        for i in range(ROWS):
            pad[1 + i, 8 + COLS : 9 + COLS, :] = colrec[n, 0, i : i + 1, :]
            pad[1 + i, 7:8, :] = colrec[n, 1, i : i + 1, :]
        last, end = ROWS + 1, 8 + COLS
        pad[last, 8:end, :] = rowrec[n, 0].astype(F32) * below
        pad[0, 8:end, :] = rowrec[n, 1].astype(F32) * above_me
        pad[last, end : end + 1, :] = colrec[n, 2, 0:1, :] * below
        pad[last, 7:8, :] = colrec[n, 3, 0:1, :] * below
        pad[0, end : end + 1, :] = colrec[n, 4, ROWS - 1 : ROWS, :] * above_me
        pad[0, 7:8, :] = colrec[n, 5, ROWS - 1 : ROWS, :] * above_me
        for b in range(3):
            for t in range(2):
                at = 7 + b + 16 * t
                shifted[b, t] = pad[:, at : at + 16, :].astype(BF16)

    def patch(a, b):
        parts = [shifted[b, t, a : a + ROWS].reshape(NPTS // 2, C) for t in range(2)]
        return jnp.concatenate(parts, axis=0)

    loads[0].wait()
    for r in range(ROWS):
        pad[1 + r, 8 : 8 + COLS, :] = fields[r].astype(F32)
    pack(0)
    rowbuf[0, 0] = fields[0]
    rowbuf[0, 1] = fields[ROWS - 1]
    pl.semaphore_wait(barrier, len(everyone))
    halo = halo_copies(0)
    for copy in halo:
        copy.start()

    for load in loads[1:4]:
        load.wait()
    lane = lax.broadcasted_iota(jnp.int32, (8, 128), 1)
    row = lax.broadcasted_iota(jnp.int32, (8, 128), 0)
    wide = jnp.concatenate([tiles_i[...].astype(F32), jnp.zeros((120, 128), F32)], axis=0)
    wide = jnp.transpose(wide)
    src_b = lax.broadcasted_iota(jnp.int32, (128, 128), 0)
    dst_r = lax.broadcasted_iota(jnp.int32, (128, 128), 1) & 31
    by_member = jnp.zeros((32, 128), F32)
    for q in range(4):
        pick = jnp.where(4 * src_b + q == dst_r, 1.0, 0.0)
        by_member = by_member + jnp.dot(
            wide[32 * q : 32 * (q + 1), :], pick,
            precision=lax.Precision.HIGHEST, preferred_element_type=F32,
        )
    quarter = lane[0:1, :] >> 5
    for blk in range(8):
        line = by_member[4 * blk : 4 * blk + 1, :]
        for j in range(1, 4):
            line = jnp.where(quarter == j, by_member[4 * blk + j : 4 * blk + j + 1, :], line)
        small[blk : blk + 1, :] = line
    small[8:16, :] = jnp.zeros((8, 128), F32)
    small[8:9, 0:NREG] = tail_i[...].astype(F32)
    small[9:10, 0:NREG] = weight_f[...]
    tails = small[8:16, :]
    tails = tails + pltpu.roll(tails, 64, 1)
    small[8:16, :] = tails + pltpu.roll(tails, 32, 1)

    def lat_weight(row_in_band):
        ids = (row_in_band + lat * ROWS).astype(F32)
        return jnp.cos(jnp.pi * (ids + 0.5) / (NLAT * ROWS) - jnp.pi / 2)

    lw8 = lat_weight(row)
    for i in range(ROWS):
        for t in range(2):
            at = 128 * t + 16 * i
            lwc[at : at + 16, :] = jnp.broadcast_to(lw8[i : i + 1, :], (16, 128))
    lw_row = lat_weight((lax.broadcasted_iota(jnp.int32, (1, NPTS), 1) >> 4) & 7)

    slot = lax.broadcasted_iota(jnp.int32, (1024, 128), 0)
    at_t, at_z, at_y = slot & 1, (slot >> 1) & 7, (slot >> 4) & 7
    at_x, at_c = (slot >> 7) & 3, slot >> 9
    tile = ((at_y >> 2) * 8 + at_z) * 64 + (at_x * 8 + (at_y & 3) * 2 + at_c) * 2 + at_t
    tile = tile.astype(F32)
    for blk in range(8):
        pt[:, 128 * blk : 128 * (blk + 1)] = jnp.where(
            tile == small[blk : blk + 1, :], 1.0, 0.0
        ).astype(BF16)

    for copy in halo:
        copy.wait()
    place(0)

    for load in loads[4:]:
        load.wait()
    pre = jnp.zeros((NPTS, C), F32)
    for a in range(3):
        for b in range(3):
            k = 3 * a + b
            pre = pre + jnp.dot(
                patch(a, b), w[k * C : (k + 1) * C, :], preferred_element_type=F32
            )
    pre = pre + bias[...]
    act, slope = gelu_pair(pre)
    aim = jnp.concatenate(
        [target[:, 16 * t : 16 * (t + 1), :].reshape(NPTS // 2, C) for t in range(2)], axis=0
    )
    diff = act - aim.astype(F32)
    ds_ref[...] = diff * slope
    square = diff * diff
    lw_col = lwc[:, 0:1]
    err_row = lax.dot_general(
        jnp.ones((8, C), F32), square, (((1,), (1,)), ((), ())),
        precision=lax.Precision.HIGHEST, preferred_element_type=F32,
    )[0:1, :] * (1.0 / C) * lw_row
    r1[z, 0:1, :] = err_row[:, :128]
    r1[z, 1:2, :] = err_row[:, 128:]

    def exchange(ref, slot_id, peers, first):
        copies = [
            remote(ref.at[slot_id], ref.at[slot_id], gsend.at[first + k], grecv.at[first + k], peer)
            for k, peer in enumerate(peers)
        ]
        for copy in copies:
            copy.start()
        return copies

    def turn(taps):
        for k in taps:
            turned[k] = jnp.transpose(patch(k // 3, k % 3))

    copies = exchange(r1, z, zs, 0)
    err_col = jnp.sum(square, axis=1, keepdims=True) * (1.0 / C) * lw_col
    turn(range(4))
    for copy in copies:
        copy.wait()
    for zz in range(NZ):
        r4[core, x, y, 2 * zz : 2 * zz + 2, :] = r1[zz, 0:2, :]
    copies = exchange(r4.at[core, x], y, ys, 7)
    turn(range(4, 9))
    for copy in copies:
        copy.wait()
    copies = exchange(r4.at[core], x, xs, 14)
    passed = exchange(r4.at[core], x, cs, 17)
    for n, k in enumerate((1, 3, 2)):
        copies[k - 1].wait()
        passed += exchange(r4.at[core], (x + NX - k) % NX, cs, 18 + n)
    for copy in passed:
        copy.wait()

    values = jnp.transpose(r4[...].reshape(1024, 128))
    high = values.astype(BF16)
    rest = values - high.astype(F32)
    mid = rest.astype(BF16)
    low = (rest - mid.astype(F32)).astype(BF16)
    three = jnp.concatenate([high, mid, low], axis=0)
    for blk in range(4):
        part = jnp.dot(three, pt[:, 256 * blk : 256 * (blk + 1)], preferred_element_type=F32)
        es[:, 256 * blk : 256 * (blk + 1)] = part[:128] + part[128:256] + part[256:]

    def fold(value):
        total = value[:, 0:128]
        for blk in range(1, 8):
            total = total + value[:, 128 * blk : 128 * (blk + 1)]
        total = jnp.sum(total, axis=0, keepdims=True)
        total = jnp.broadcast_to(total, (8, 128))
        total = total + pltpu.roll(total, 64, 1)
        return total + pltpu.roll(total, 32, 1)

    points = float(NPTS // 2 * 32)
    count = jnp.broadcast_to(small[8:9, :], (8, 128))
    weight = jnp.broadcast_to(small[9:10, :], (8, 128))

    def lanes(thresh):
        return jnp.concatenate([thresh[0:1, :]] * 8, axis=1)

    thresh = 2.0 * fold(es[...]) / points

    def iterate(_, thresh):
        half = (es[...] - lanes(thresh)) * (0.5 / SMOOTH)
        tangent = jnp.tanh(half)
        above = 0.5 * (fold(tangent) + points)
        spread = 0.25 * fold(1.0 - tangent * tangent)
        return thresh + jnp.clip(
            DAMPING * SMOOTH * (above - count) / (spread + 1.0), -STEP_LIMIT, STEP_LIMIT
        )

    thresh = lax.fori_loop(0, ITERS, iterate, thresh)

    numbers = small[0:8, :]
    ratio = weight / count
    half_rows = lax.broadcasted_iota(jnp.int32, (NPTS, 1), 0) < NPTS // 2
    own_thresh, own_ratio = [], []
    for t in range(2):
        mine = numbers == (lat * 64 + lon * 2 + t).astype(F32)
        for source, sink in ((thresh, own_thresh), (ratio, own_ratio)):
            picked = jnp.where(mine, source, 0.0)
            sink.append(jnp.sum(jnp.sum(picked, axis=0, keepdims=True), axis=1, keepdims=True))
    my_thresh = jnp.where(half_rows, own_thresh[0], own_thresh[1])
    my_ratio = jnp.where(half_rows, own_ratio[0], own_ratio[1])
    sig = 1.0 / (1.0 + jnp.exp((my_thresh - err_col) * (1.0 / SMOOTH)))
    d_err = my_ratio * sig * lw_col
    gp = ((d_err * (2.0 / C)) * ds_ref[...]).astype(BF16)
    for t in range(2):
        piece = gp[t * 128 : (t + 1) * 128, :].reshape(ROWS, 16, C)
        pad[1 : 1 + ROWS, 8 + 16 * t : 24 + 16 * t, :] = piece.astype(F32)
        rowbuf[1, 0, 16 * t : 16 * (t + 1), :] = piece[0]
        rowbuf[1, 1, 16 * t : 16 * (t + 1), :] = piece[ROWS - 1]
    pack(1)
    halo = halo_copies(1)
    for copy in halo:
        copy.start()

    gb0[core] = jnp.sum(gp.astype(F32), axis=0, keepdims=True)

    def taps(which):
        for k in which:
            tap = jnp.dot(turned[k], gp, preferred_element_type=F32)
            if k == 4:
                gk[0, 1024:1152, :] = tap[0:128]
                gk[1, 0:128, :] = tap[128:256]
            elif k < 4:
                gk[0, k * C : (k + 1) * C, :] = tap
            else:
                at = k * C - 1152
                gk[1, at : at + C, :] = tap

    used = [0]

    def send(src, dst, peer):
        n = used[0]
        used[0] += 1
        copy = remote(src, dst, asend.at[n], arecv.at[n], peer)
        copy.start()
        return copy

    def wait(copies):
        for copy in copies:
            copy.wait()

    def share(ref, slot_id, peers):
        return [send(ref.at[slot_id], ref.at[slot_id], peer) for peer in peers]

    def scatter(src, dst, me, count, peers):
        return [
            send(src.at[(me + k) % count], dst.at[k - 1], peer)
            for k, peer in zip(range(1, count), peers)
        ]

    spans = {"x": (0, 512), "y": (512, 896), "z": (896, 1152)}

    def to_other_core(name):
        low, high = spans[name]
        cbuf[low:high, :] = gk[1 - core, low:high, :].astype(BF16)
        return [send(cbuf.at[low:high], crec.at[low:high], cs[0])]

    taps((2, 3, 6, 7))
    paired_y = to_other_core("y")
    taps((0, 1, 4, 5))
    paired_x = to_other_core("x")
    taps((8,))
    paired_z = to_other_core("z") + share(gb0, core, cs)

    def split(name, parts, sends, size):
        for n in range(parts.shape[0]):
            at = spans[name][0] + n * size
            chunk = gk[core, at : at + size, :] + crec[at : at + size, :].astype(F32)
            parts[n] = chunk
            sends[n] = chunk.astype(BF16)

    wait(paired_y)
    split("y", hy, sy, 48)
    first_y = scatter(sy, ry, y, NY, ys)
    wait(paired_x)
    split("x", hx, sx, 128)
    first_x = scatter(sx, rx, x, NX, xs)
    wait(paired_z)
    split("z", hz, sz, 32)
    first_z = scatter(sz, rz, z, NZ, zs)
    gbx[x] = gb0[0] + gb0[1]
    first_x += share(gbx, x, xs)

    wait(halo)
    place(1)
    total = jnp.zeros((NPTS, C), F32)
    for a in range(3):
        for b in range(3):
            k = 3 * a + b
            total = total + lax.dot_general(
                patch(2 - a, 2 - b), w[k * C : (k + 1) * C, :],
                (((1,), (1,)), ((), ())), preferred_element_type=F32,
            )
    total = total.astype(BF16)
    for t in range(2):
        gf_out[:, 16 * t : 16 * (t + 1), :] = total[t * 128 : (t + 1) * 128].reshape(ROWS, 16, C)

    scaled = (es[...] - lanes(thresh)) * (1.0 / SMOOTH)
    soft = jnp.maximum(scaled, 0.0) + jnp.log1p(jnp.exp(-jnp.abs(scaled)))
    rl_out[...] = (thresh + SMOOTH * fold(soft) / count)[0:1, 0:NREG]

    def gathered(own, received):
        for n in range(received.shape[0]):
            own = own + received[n].astype(F32)
        return own

    def in_order(ref):
        value = ref[0].astype(F32)
        for n in range(1, ref.shape[0]):
            value = value + ref[n].astype(F32)
        return value

    wait(first_x)
    part = gathered(hx[x], rx)
    for n in range(NY):
        hx2[n] = part[16 * n : 16 * (n + 1), :]
        sx2[n] = part[16 * n : 16 * (n + 1), :].astype(BF16)
    gby[y] = in_order(gbx)
    second_x = scatter(sx2, rx2, y, NY, ys) + share(gby, y, ys)

    wait(first_z)
    part = gathered(hz[z], rz)
    for n in range(NX):
        sz2[n] = part[8 * n : 8 * (n + 1), :]
    second_z = scatter(sz2, rz2, x, NX, xs)

    wait(first_y)
    hy[y] = gathered(hy[y], ry)
    for n in range(NZ):
        sy2[n, 0:6, :] = hy[y, 6 * n : 6 * n + 6, :]
        sy2[n, 6:8, :] = jnp.zeros((2, C), F32)
    second_y = scatter(sy2, ry2, z, NZ, zs)

    wait(second_x)
    ex[z] = gathered(hx2[y], rx2).astype(BF16)
    gbz[z] = in_order(gby)
    third_x = share(ex, z, zs) + share(gbz, z, zs)
    wait(second_z)
    ez[y] = gathered(sz2[x], rz2)
    third_z = share(ez, y, ys)
    wait(second_y)
    ey[x] = gathered(sy2[z], ry2)
    third_y = share(ey, x, xs)

    wait(third_x)
    at = pl.multiple_of(128 * x + 16 * y, 16)
    gk_out[core, pl.ds(at, 16), :] = in_order(ex).astype(BF16)
    mine = gk_out.at[core, pl.ds(at, 16)]
    fourth_x = [send(mine, mine, peer) for peer in ys]
    gb_out[...] = in_order(gbz)
    wait(third_y)
    fy[z] = in_order(ey)
    fourth_y = share(fy, z, zs)
    wait(third_z)
    fz[x] = in_order(ez)
    fourth_z = share(fz, x, xs)

    def spread_out(at, size, peers):
        mine = gk_out.at[core, pl.ds(at, size)]
        return [send(mine, mine, peer) for peer in peers]

    def hand_over(name):
        low, high = spans[name]
        mine = gk_out.at[core, low:high]
        return [send(mine, mine, cs[0])]

    wait(fourth_z)
    at_z = pl.multiple_of(896 + 32 * z, 16)
    gk_out[core, pl.ds(at_z, 32), :] = fz[...].reshape(32, C).astype(BF16)
    fifth_z = spread_out(at_z, 32, zs)
    wait(fourth_y)
    for n in range(NZ):
        hy[y, 6 * n : 6 * n + 6, :] = fy[n, 0:6, :]
    at_y = pl.multiple_of(512 + 48 * y, 16)
    gk_out[core, pl.ds(at_y, 48), :] = hy[y].astype(BF16)
    fifth_y = spread_out(at_y, 48, ys)
    wait(fourth_x)
    fifth_x = spread_out(pl.multiple_of(128 * x, 128), 128, xs)
    wait(fifth_z)
    last = hand_over("z")
    wait(fifth_x)
    last += hand_over("x")
    wait(fifth_y)
    last += hand_over("y")
    wait(last)


def leave(gf, gk, gb, rl, gf_out, gk_out, gb_out, rl_out, gf_v, gk_v, gb_v, rl_v, sems):
    half = gk.shape[1] // 2
    trips = [(gf, gf_v, gf_out), (gb, gb_v, gb_out), (rl, rl_v, rl_out)]
    for h in range(2):
        for low in (0, half):
            span = pl.ds(low, half)
            trips.append((gk.at[h, span], gk_v.at[h, span], gk_out.at[h, span]))
    arrive = [pltpu.make_async_copy(a, b, sems.at[0, n]) for n, (a, b, _) in enumerate(trips)]
    depart = [pltpu.make_async_copy(b, c, sems.at[1, n]) for n, (_, b, c) in enumerate(trips)]
    for copy in arrive:
        copy.start()
    for first, second in zip(arrive, depart):
        first.wait()
        second.start()
    for copy in depart:
        copy.wait()


def on_device(fields, kernel, bias, target, tile_list, tail_count, region_weight):
    vmem = pl.BlockSpec(memory_space=pltpu.VMEM)
    dma = pltpu.SemaphoreType.DMA
    v = pltpu.VMEM
    gf, gk, gb, rl = pl.pallas_call(
        body,
        out_shape=(
            jax.ShapeDtypeStruct((ROWS, COLS, C), BF16),
            jax.ShapeDtypeStruct((2, 1152, C), BF16),
            jax.ShapeDtypeStruct((1, C), F32),
            jax.ShapeDtypeStruct((1, NREG), F32),
        ),
        in_specs=[pl.BlockSpec(memory_space=pl.ANY)] * 7,
        out_specs=(vmem,) * 4,
        scratch_shapes=[
            v((ROWS, COLS, C), BF16), v((9 * C, C), BF16), v((1, C), F32), v((ROWS, COLS, C), BF16),
            v((8, 128), jnp.int32), v((1, NREG), jnp.int32), v((1, NREG), F32),
            v((16, 128), F32), v((NPTS, 128), F32),
            v((ROWS + 2, 48, C), F32), v((3, 2, ROWS + 2, 16, C), BF16), v((9, C, NPTS), BF16),
            v((2, 2, ROWS, C), F32), v((2, 2, COLS, C), BF16),
            v((2, 6, ROWS, C), F32), v((2, 2, COLS, C), BF16),
            v((NPTS, C), F32), v((NZ, 8, 128), F32), v((2, NX, NY, 16, 128), F32),
            v((1024, 1024), BF16), v((128, 1024), F32),
            v((2, 1152, C), F32), v((1152, C), BF16), v((1152, C), BF16),
            v((NX, 128, C), F32), v((NY, 48, C), F32), v((NZ, 32, C), F32),
            v((NX, 128, C), BF16), v((NY, 48, C), BF16), v((NZ, 32, C), BF16),
            v((NX - 1, 128, C), BF16), v((NY - 1, 48, C), BF16), v((NZ - 1, 32, C), BF16),
            v((NY, 16, C), F32), v((NY, 16, C), BF16), v((NY - 1, 16, C), BF16),
            v((NZ, 8, C), F32), v((NZ - 1, 8, C), F32),
            v((NX, 8, C), F32), v((NX - 1, 8, C), F32),
            v((NZ, 16, C), BF16), v((NX, 8, C), F32), v((NY, 8, C), F32),
            v((NZ, 8, C), F32), v((NX, 8, C), F32),
            v((2, 1, C), F32), v((NX, 1, C), F32), v((NY, 1, C), F32), v((NZ, 1, C), F32),
            dma((7,)), dma((2, 8)), dma((2, 8)), dma((21,)), dma((21,)), dma((110,)), dma((110,)),
        ],
        compiler_params=pltpu.CompilerParams(
            collective_id=0, has_side_effects=True, vmem_limit_bytes=60 * 1024 * 1024
        ),
        name="layer",
    )(
        fields, kernel.reshape(9 * C, C), bias.reshape(1, C), target,
        tile_list.reshape(8, 128), tail_count.reshape(1, NREG), region_weight.reshape(1, NREG),
    )
    results = (gf, gk, gb, rl)
    anywhere = pl.BlockSpec(memory_space=pl.ANY)
    gf, gk, gb, rl = pl.pallas_call(
        leave,
        out_shape=[jax.ShapeDtypeStruct(r.shape, r.dtype) for r in results],
        in_specs=[anywhere] * 4,
        out_specs=[anywhere] * 4,
        scratch_shapes=[pltpu.VMEM(r.shape, r.dtype) for r in results] + [dma((2, 7))],
        name="leave",
    )(*results)
    return gf, gk.reshape(3, 3, C, C), gb.reshape(C), rl.reshape(NREG)


def solution(mesh):
    placed = (P("lat", "lon", None), P(), P(), P("lat", "lon", None), P(), P(), P())
    return jax.shard_map(
        on_device,
        mesh=mesh,
        in_specs=placed,
        out_specs=(P("lat", "lon", None), P(), P(), P()),
        check_vma=False,
    )
```

```python
import functools

import jax
import jax.numpy as jnp
from jax import lax
from jax.experimental import pallas as pl
from jax.experimental.pallas import tpu as pltpu
from jax.sharding import PartitionSpec as P

NREG = 32
ITERS = 6
SMOOTH = 0.05
STEP_LIMIT = 0.3
DAMPING = 0.4
GELU_SCALE = 0.7978845608
GELU_CUBIC = 0.044715

MESH = pl.DeviceIdType.MESH
NLAT, NLON = 16, 32
NX, NY, NZ = 4, 8, 8
ROWS, COLS, C = 8, 32, 256
NPTS = ROWS * COLS
F32, BF16 = jnp.float32, jnp.bfloat16


def gelu_pair(value):
    inner = GELU_SCALE * (value + GELU_CUBIC * value * value * value)
    tangent = jnp.tanh(inner)
    act = 0.5 * value * (1.0 + tangent)
    slope = 0.5 * (1.0 + tangent) + 0.5 * value * (1.0 - tangent * tangent) * GELU_SCALE * (
        1.0 + 3.0 * GELU_CUBIC * value * value
    )
    return act, slope


def position():
    lat, lon = lax.axis_index("lat"), lax.axis_index("lon")
    x, y, z, core = lon // 8, (lat // 8) * 4 + (lon % 8) // 2, lat % 8, lon % 2
    return lat, lon, x, y, z, core


def device_at(x, y, z, core):
    return ((y // 4) * 8 + z, x * 8 + (y % 4) * 2 + core)


def halo_peers(lat, lon):
    steps = ((0, -1), (0, 1), (-1, 0), (1, 0), (-1, -1), (-1, 1), (1, -1), (1, 1))
    return [((lat + dl + NLAT) % NLAT, (lon + dn + NLON) % NLON) for dl, dn in steps]


def line_peers(x, y, z, core):
    zs = [device_at(x, y, (z + k) % NZ, core) for k in range(1, NZ)]
    ys = [device_at(x, (y + k) % NY, z, core) for k in range(1, NY)]
    xs = [device_at((x + k) % NX, y, z, core) for k in range(1, NX)]
    return zs, ys, xs, [device_at(x, y, z, 1 - core)]


FAR_FIRST = (4, 3, 5, 2, 6, 1, 7, 0)


def plane_peers(x, y, z, core):
    steps = [(dy, dz) for dz in FAR_FIRST for dy in FAR_FIRST if (dy, dz) != (0, 0)]
    return [device_at(x, (y + dy) % NY, (z + dz) % NZ, core) for dy, dz in steps]


def body(fields_hbm, w_hbm, bias_hbm, target_hbm, list_hbm, tail_hbm, weight_hbm,
         gf_out, gk_out, gb_out, rl_out,
         fields, w, bias, target, tiles_i, tail_i, weight_f, small, lwc,
         pad, shifted, turned, colbuf, rowbuf, colrec, rowrec, ds_ref, r1, r4, pt, es,
         gk, cbuf, crec, hx, hy, hz, sx, sy, sz, rx, ry, rz,
         hx2, sx2, rx2, sy2, ry2, sz2, rz2, ex, ey, ez, fy, fz, gb0, gbx, gby, gbz,
         plane_sem, lsem, hsend, hrecv, gsend, grecv, asend, arecv):
    lat, lon, x, y, z, core = position()
    loads = [
        pltpu.make_async_copy(src, dst, lsem.at[n])
        for n, (src, dst) in enumerate((
            (fields_hbm, fields), (list_hbm, tiles_i), (tail_hbm, tail_i),
            (weight_hbm, weight_f), (w_hbm, w), (bias_hbm, bias), (target_hbm, target),
        ))
    ]
    for load in loads:
        load.start()
    zs, ys, xs, cs = line_peers(x, y, z, core)
    halos = halo_peers(lat, lon)

    barrier = pltpu.get_barrier_semaphore()
    everyone = halos + zs + ys + xs + cs
    for peer in everyone:
        pl.semaphore_signal(barrier, inc=1, device_id=peer, device_id_type=MESH)

    def remote(src, dst, send, recv, peer):
        return pltpu.make_async_remote_copy(
            src_ref=src, dst_ref=dst, send_sem=send, recv_sem=recv,
            device_id=peer, device_id_type=MESH,
        )

    def pack(n):
        for i in range(ROWS):
            colbuf[n, 0, i : i + 1, :] = pad[1 + i, 8:9, :]
            colbuf[n, 1, i : i + 1, :] = pad[1 + i, 7 + COLS : 8 + COLS, :]

    def halo_copies(n):
        west, east = colbuf.at[n, 0], colbuf.at[n, 1]
        north, south = rowbuf.at[n, 0], rowbuf.at[n, 1]
        sources = (west, east, north, south, west, east, west, east)
        targets = (
            colrec.at[n, 0], colrec.at[n, 1], rowrec.at[n, 0], rowrec.at[n, 1],
            colrec.at[n, 2], colrec.at[n, 3], colrec.at[n, 4], colrec.at[n, 5],
        )
        return [
            remote(sources[d], targets[d], hsend.at[n, d], hrecv.at[n, d], halos[d])
            for d in range(8)
        ]

    below = (lat < NLAT - 1).astype(F32)
    above_me = (lat > 0).astype(F32)

    def place(n):
        for i in range(ROWS):
            pad[1 + i, 8 + COLS : 9 + COLS, :] = colrec[n, 0, i : i + 1, :]
            pad[1 + i, 7:8, :] = colrec[n, 1, i : i + 1, :]
        last, end = ROWS + 1, 8 + COLS
        pad[last, 8:end, :] = rowrec[n, 0].astype(F32) * below
        pad[0, 8:end, :] = rowrec[n, 1].astype(F32) * above_me
        pad[last, end : end + 1, :] = colrec[n, 2, 0:1, :] * below
        pad[last, 7:8, :] = colrec[n, 3, 0:1, :] * below
        pad[0, end : end + 1, :] = colrec[n, 4, ROWS - 1 : ROWS, :] * above_me
        pad[0, 7:8, :] = colrec[n, 5, ROWS - 1 : ROWS, :] * above_me
        for b in range(3):
            for t in range(2):
                at = 7 + b + 16 * t
                shifted[b, t] = pad[:, at : at + 16, :].astype(BF16)

    def patch(a, b):
        parts = [shifted[b, t, a : a + ROWS].reshape(NPTS // 2, C) for t in range(2)]
        return jnp.concatenate(parts, axis=0)

    loads[0].wait()
    for r in range(ROWS):
        pad[1 + r, 8 : 8 + COLS, :] = fields[r].astype(F32)
    pack(0)
    rowbuf[0, 0] = fields[0]
    rowbuf[0, 1] = fields[ROWS - 1]
    pl.semaphore_wait(barrier, len(everyone))
    halo = halo_copies(0)
    for copy in halo:
        copy.start()
    for peer in ys:
        pl.semaphore_signal(plane_sem, inc=1, device_id=peer, device_id_type=MESH)

    for load in loads[1:4]:
        load.wait()
    lane = lax.broadcasted_iota(jnp.int32, (8, 128), 1)
    row = lax.broadcasted_iota(jnp.int32, (8, 128), 0)
    wide = jnp.concatenate([tiles_i[...].astype(F32), jnp.zeros((120, 128), F32)], axis=0)
    wide = jnp.transpose(wide)
    src_b = lax.broadcasted_iota(jnp.int32, (128, 128), 0)
    dst_r = lax.broadcasted_iota(jnp.int32, (128, 128), 1) & 31
    by_member = jnp.zeros((32, 128), F32)
    for q in range(4):
        pick = jnp.where(4 * src_b + q == dst_r, 1.0, 0.0)
        by_member = by_member + jnp.dot(
            wide[32 * q : 32 * (q + 1), :], pick,
            precision=lax.Precision.HIGHEST, preferred_element_type=F32,
        )
    quarter = lane[0:1, :] >> 5
    for blk in range(8):
        line = by_member[4 * blk : 4 * blk + 1, :]
        for j in range(1, 4):
            line = jnp.where(quarter == j, by_member[4 * blk + j : 4 * blk + j + 1, :], line)
        small[blk : blk + 1, :] = line
    small[8:16, :] = jnp.zeros((8, 128), F32)
    small[8:9, 0:NREG] = tail_i[...].astype(F32)
    small[9:10, 0:NREG] = weight_f[...]
    tails = small[8:16, :]
    tails = tails + pltpu.roll(tails, 64, 1)
    small[8:16, :] = tails + pltpu.roll(tails, 32, 1)

    def lat_weight(row_in_band):
        ids = (row_in_band + lat * ROWS).astype(F32)
        return jnp.cos(jnp.pi * (ids + 0.5) / (NLAT * ROWS) - jnp.pi / 2)

    lw8 = lat_weight(row)
    for i in range(ROWS):
        for t in range(2):
            at = 128 * t + 16 * i
            lwc[at : at + 16, :] = jnp.broadcast_to(lw8[i : i + 1, :], (16, 128))
    lw_row = lat_weight((lax.broadcasted_iota(jnp.int32, (1, NPTS), 1) >> 4) & 7)

    slot = lax.broadcasted_iota(jnp.int32, (1024, 128), 0)
    at_t, at_y, at_z = (slot >> 6) & 1, (slot >> 3) & 7, slot & 7
    at_x, at_c = (slot >> 7) & 3, slot >> 9
    tile = ((at_y >> 2) * 8 + at_z) * 64 + (at_x * 8 + (at_y & 3) * 2 + at_c) * 2 + at_t
    tile = tile.astype(F32)
    for blk in range(8):
        pt[:, 128 * blk : 128 * (blk + 1)] = jnp.where(
            tile == small[blk : blk + 1, :], 1.0, 0.0
        ).astype(BF16)

    for copy in halo:
        copy.wait()
    place(0)

    for load in loads[4:]:
        load.wait()
    pre = jnp.zeros((NPTS, C), F32)
    for a in range(3):
        for b in range(3):
            k = 3 * a + b
            pre = pre + jnp.dot(
                patch(a, b), w[k * C : (k + 1) * C, :], preferred_element_type=F32
            )
    pre = pre + bias[...]
    act, slope = gelu_pair(pre)
    aim = jnp.concatenate(
        [target[:, 16 * t : 16 * (t + 1), :].reshape(NPTS // 2, C) for t in range(2)], axis=0
    )
    diff = act - aim.astype(F32)
    ds_ref[...] = diff * slope
    square = diff * diff
    lw_col = lwc[:, 0:1]
    err_row = lax.dot_general(
        jnp.ones((8, C), F32), square, (((1,), (1,)), ((), ())),
        precision=lax.Precision.HIGHEST, preferred_element_type=F32,
    )[0:1, :] * (1.0 / C) * lw_row
    r1[8 * y + z] = err_row

    def exchange(ref, slot_id, peers, first):
        copies = [
            remote(ref.at[slot_id], ref.at[slot_id], gsend.at[first + k], grecv.at[first + k], peer)
            for k, peer in enumerate(peers)
        ]
        for copy in copies:
            copy.start()
        return copies

    def turn(taps):
        for k in taps:
            turned[k] = jnp.transpose(patch(k // 3, k % 3))

    pl.semaphore_wait(plane_sem, NY - 1)
    copies = exchange(r1, 8 * y + z, plane_peers(x, y, z, core), 0)
    err_col = jnp.sum(square, axis=1, keepdims=True) * (1.0 / C) * lw_col
    turn(range(9))
    for copy in copies:
        copy.wait()
    for n in range(NY * NZ):
        r4[core, x, n : n + 1, :] = r1[n, :, :128]
        r4[core, x, 64 + n : 65 + n, :] = r1[n, :, 128:]
    copies = exchange(r4.at[core], x, xs, 63)
    passed = exchange(r4.at[core], x, cs, 66)
    for n, k in enumerate((1, 3, 2)):
        copies[k - 1].wait()
        passed += exchange(r4.at[core], (x + NX - k) % NX, cs, 67 + n)
    for copy in passed:
        copy.wait()

    values = jnp.transpose(r4[...].reshape(1024, 128))
    high = values.astype(BF16)
    rest = values - high.astype(F32)
    mid = rest.astype(BF16)
    low = (rest - mid.astype(F32)).astype(BF16)
    three = jnp.concatenate([high, mid, low], axis=0)
    for blk in range(4):
        part = jnp.dot(three, pt[:, 256 * blk : 256 * (blk + 1)], preferred_element_type=F32)
        es[:, 256 * blk : 256 * (blk + 1)] = part[:128] + part[128:256] + part[256:]

    def everywhere(total):
        for shift in (4, 2, 1):
            total = total + pltpu.roll(total, shift, 0)
        total = total + pltpu.roll(total, 64, 1)
        return total + pltpu.roll(total, 32, 1)

    def over_points(terms):
        totals = None
        for blk in range(8):
            block = es[:, 128 * blk : 128 * (blk + 1)].reshape(16, 8, 128)
            sums = [jnp.sum(term, axis=0) for term in terms(block)]
            totals = sums if totals is None else [a + b for a, b in zip(totals, sums)]
        return [everywhere(total) for total in totals]

    points = float(NPTS // 2 * 32)
    count = jnp.broadcast_to(small[8:9, :], (8, 128))
    weight = jnp.broadcast_to(small[9:10, :], (8, 128))

    thresh = 2.0 * over_points(lambda block: [block])[0] / points

    def iterate(_, thresh):
        def terms(block):
            tangent = jnp.tanh((block - thresh) * (0.5 / SMOOTH))
            return [tangent, 1.0 - tangent * tangent]

        tangents, spreads = over_points(terms)
        above = 0.5 * (tangents + points)
        return thresh + jnp.clip(
            DAMPING * SMOOTH * (above - count) / (0.25 * spreads + 1.0), -STEP_LIMIT, STEP_LIMIT
        )

    thresh = lax.fori_loop(0, ITERS, iterate, thresh)

    numbers = small[0:8, :]
    ratio = weight / count
    half_rows = lax.broadcasted_iota(jnp.int32, (NPTS, 1), 0) < NPTS // 2
    own_thresh, own_ratio = [], []
    for t in range(2):
        mine = numbers == (lat * 64 + lon * 2 + t).astype(F32)
        for source, sink in ((thresh, own_thresh), (ratio, own_ratio)):
            picked = jnp.where(mine, source, 0.0)
            sink.append(jnp.sum(jnp.sum(picked, axis=0, keepdims=True), axis=1, keepdims=True))
    my_thresh = jnp.where(half_rows, own_thresh[0], own_thresh[1])
    my_ratio = jnp.where(half_rows, own_ratio[0], own_ratio[1])
    sig = 1.0 / (1.0 + jnp.exp((my_thresh - err_col) * (1.0 / SMOOTH)))
    d_err = my_ratio * sig * lw_col
    gp = ((d_err * (2.0 / C)) * ds_ref[...]).astype(BF16)
    for t in range(2):
        piece = gp[t * 128 : (t + 1) * 128, :].reshape(ROWS, 16, C)
        pad[1 : 1 + ROWS, 8 + 16 * t : 24 + 16 * t, :] = piece.astype(F32)
        rowbuf[1, 0, 16 * t : 16 * (t + 1), :] = piece[0]
        rowbuf[1, 1, 16 * t : 16 * (t + 1), :] = piece[ROWS - 1]
    pack(1)
    halo = halo_copies(1)
    for copy in halo:
        copy.start()

    gb0[core] = jnp.sum(gp.astype(F32), axis=0, keepdims=True)

    def taps(which):
        for k in which:
            tap = jnp.dot(turned[k], gp, preferred_element_type=F32)
            if k == 4:
                gk[0, 1024:1152, :] = tap[0:128]
                gk[1, 0:128, :] = tap[128:256]
            elif k < 4:
                gk[0, k * C : (k + 1) * C, :] = tap
            else:
                at = k * C - 1152
                gk[1, at : at + C, :] = tap

    used = [0]

    def send(src, dst, peer):
        n = used[0]
        used[0] += 1
        copy = remote(src, dst, asend.at[n], arecv.at[n], peer)
        copy.start()
        return copy

    def wait(copies):
        for copy in copies:
            copy.wait()

    def share(ref, slot_id, peers):
        return [send(ref.at[slot_id], ref.at[slot_id], peer) for peer in peers]

    def scatter(src, dst, me, count, peers):
        return [
            send(src.at[(me + k) % count], dst.at[k - 1], peer)
            for k, peer in zip(range(1, count), peers)
        ]

    spans = {"x": (0, 512), "y": (512, 896), "z": (896, 1152)}

    def to_other_core(name):
        low, high = spans[name]
        cbuf[low:high, :] = gk[1 - core, low:high, :].astype(BF16)
        return [send(cbuf.at[low:high], crec.at[low:high], cs[0])]

    taps((2, 3, 6, 7))
    paired_y = to_other_core("y")
    taps((0, 1, 4, 5))
    paired_x = to_other_core("x")
    taps((8,))
    paired_z = to_other_core("z") + share(gb0, core, cs)

    def split(name, parts, sends, size):
        for n in range(parts.shape[0]):
            at = spans[name][0] + n * size
            chunk = gk[core, at : at + size, :] + crec[at : at + size, :].astype(F32)
            parts[n] = chunk
            sends[n] = chunk.astype(BF16)

    wait(paired_y)
    split("y", hy, sy, 48)
    first_y = scatter(sy, ry, y, NY, ys)
    wait(paired_x)
    split("x", hx, sx, 128)
    first_x = scatter(sx, rx, x, NX, xs)
    wait(paired_z)
    split("z", hz, sz, 32)
    first_z = scatter(sz, rz, z, NZ, zs)
    gbx[x] = gb0[0] + gb0[1]
    first_x += share(gbx, x, xs)

    wait(halo)
    place(1)
    total = jnp.zeros((NPTS, C), F32)
    for a in range(3):
        for b in range(3):
            k = 3 * a + b
            total = total + lax.dot_general(
                patch(2 - a, 2 - b), w[k * C : (k + 1) * C, :],
                (((1,), (1,)), ((), ())), preferred_element_type=F32,
            )
    total = total.astype(BF16)
    for t in range(2):
        gf_out[:, 16 * t : 16 * (t + 1), :] = total[t * 128 : (t + 1) * 128].reshape(ROWS, 16, C)

    def softplus(block):
        scaled = (block - thresh) * (1.0 / SMOOTH)
        return [jnp.maximum(scaled, 0.0) + jnp.log1p(jnp.exp(-jnp.abs(scaled)))]

    soft = over_points(softplus)[0]
    rl_out[...] = (thresh + SMOOTH * soft / count)[0:1, 0:NREG]

    def gathered(own, received):
        for n in range(received.shape[0]):
            own = own + received[n].astype(F32)
        return own

    def in_order(ref):
        value = ref[0].astype(F32)
        for n in range(1, ref.shape[0]):
            value = value + ref[n].astype(F32)
        return value

    wait(first_x)
    part = gathered(hx[x], rx)
    for n in range(NY):
        hx2[n] = part[16 * n : 16 * (n + 1), :]
        sx2[n] = part[16 * n : 16 * (n + 1), :].astype(BF16)
    gby[y] = in_order(gbx)
    second_x = scatter(sx2, rx2, y, NY, ys) + share(gby, y, ys)

    wait(first_z)
    part = gathered(hz[z], rz)
    for n in range(NX):
        sz2[n] = part[8 * n : 8 * (n + 1), :]
    second_z = scatter(sz2, rz2, x, NX, xs)

    wait(first_y)
    hy[y] = gathered(hy[y], ry)
    for n in range(NZ):
        sy2[n, 0:6, :] = hy[y, 6 * n : 6 * n + 6, :]
        sy2[n, 6:8, :] = jnp.zeros((2, C), F32)
    second_y = scatter(sy2, ry2, z, NZ, zs)

    wait(second_x)
    ex[z] = gathered(hx2[y], rx2).astype(BF16)
    gbz[z] = in_order(gby)
    third_x = share(ex, z, zs) + share(gbz, z, zs)
    wait(second_z)
    ez[y] = gathered(sz2[x], rz2)
    third_z = share(ez, y, ys)
    wait(second_y)
    ey[x] = gathered(sy2[z], ry2)
    third_y = share(ey, x, xs)

    wait(third_x)
    at = pl.multiple_of(128 * x + 16 * y, 16)
    gk_out[core, pl.ds(at, 16), :] = in_order(ex).astype(BF16)
    mine = gk_out.at[core, pl.ds(at, 16)]
    fourth_x = [send(mine, mine, peer) for peer in ys]
    gb_out[...] = in_order(gbz)
    wait(third_y)
    fy[z] = in_order(ey)
    fourth_y = share(fy, z, zs)
    wait(third_z)
    fz[x] = in_order(ez)
    fourth_z = share(fz, x, xs)

    def spread_out(at, size, peers):
        mine = gk_out.at[core, pl.ds(at, size)]
        return [send(mine, mine, peer) for peer in peers]

    def hand_over(name):
        low, high = spans[name]
        mine = gk_out.at[core, low:high]
        return [send(mine, mine, cs[0])]

    wait(fourth_z)
    at_z = pl.multiple_of(896 + 32 * z, 16)
    gk_out[core, pl.ds(at_z, 32), :] = fz[...].reshape(32, C).astype(BF16)
    fifth_z = spread_out(at_z, 32, zs)
    wait(fourth_y)
    for n in range(NZ):
        hy[y, 6 * n : 6 * n + 6, :] = fy[n, 0:6, :]
    at_y = pl.multiple_of(512 + 48 * y, 16)
    gk_out[core, pl.ds(at_y, 48), :] = hy[y].astype(BF16)
    fifth_y = spread_out(at_y, 48, ys)
    wait(fourth_x)
    fifth_x = spread_out(pl.multiple_of(128 * x, 128), 128, xs)
    wait(fifth_z)
    last = hand_over("z")
    wait(fifth_x)
    last += hand_over("x")
    wait(fifth_y)
    last += hand_over("y")
    wait(last)


def leave(gf, gk, gb, rl, gf_out, gk_out, gb_out, rl_out, gf_v, gk_v, gb_v, rl_v, sems):
    half = gk.shape[1] // 2
    trips = [(gf, gf_v, gf_out), (gb, gb_v, gb_out), (rl, rl_v, rl_out)]
    for h in range(2):
        for low in (0, half):
            span = pl.ds(low, half)
            trips.append((gk.at[h, span], gk_v.at[h, span], gk_out.at[h, span]))
    arrive = [pltpu.make_async_copy(a, b, sems.at[0, n]) for n, (a, b, _) in enumerate(trips)]
    depart = [pltpu.make_async_copy(b, c, sems.at[1, n]) for n, (_, b, c) in enumerate(trips)]
    for copy in arrive:
        copy.start()
    for first, second in zip(arrive, depart):
        first.wait()
        second.start()
    for copy in depart:
        copy.wait()


def on_device(fields, kernel, bias, target, tile_list, tail_count, region_weight):
    vmem = pl.BlockSpec(memory_space=pltpu.VMEM)
    dma = pltpu.SemaphoreType.DMA
    v = pltpu.VMEM
    gf, gk, gb, rl = pl.pallas_call(
        body,
        out_shape=(
            jax.ShapeDtypeStruct((ROWS, COLS, C), BF16),
            jax.ShapeDtypeStruct((2, 1152, C), BF16),
            jax.ShapeDtypeStruct((1, C), F32),
            jax.ShapeDtypeStruct((1, NREG), F32),
        ),
        in_specs=[pl.BlockSpec(memory_space=pl.ANY)] * 7,
        out_specs=(vmem,) * 4,
        scratch_shapes=[
            v((ROWS, COLS, C), BF16), v((9 * C, C), BF16), v((1, C), F32), v((ROWS, COLS, C), BF16),
            v((8, 128), jnp.int32), v((1, NREG), jnp.int32), v((1, NREG), F32),
            v((16, 128), F32), v((NPTS, 128), F32),
            v((ROWS + 2, 48, C), F32), v((3, 2, ROWS + 2, 16, C), BF16), v((9, C, NPTS), BF16),
            v((2, 2, ROWS, C), F32), v((2, 2, COLS, C), BF16),
            v((2, 6, ROWS, C), F32), v((2, 2, COLS, C), BF16),
            v((NPTS, C), F32), v((NY * NZ, 1, 256), F32), v((2, NX, 128, 128), F32),
            v((1024, 1024), BF16), v((128, 1024), F32),
            v((2, 1152, C), F32), v((1152, C), BF16), v((1152, C), BF16),
            v((NX, 128, C), F32), v((NY, 48, C), F32), v((NZ, 32, C), F32),
            v((NX, 128, C), BF16), v((NY, 48, C), BF16), v((NZ, 32, C), BF16),
            v((NX - 1, 128, C), BF16), v((NY - 1, 48, C), BF16), v((NZ - 1, 32, C), BF16),
            v((NY, 16, C), F32), v((NY, 16, C), BF16), v((NY - 1, 16, C), BF16),
            v((NZ, 8, C), F32), v((NZ - 1, 8, C), F32),
            v((NX, 8, C), F32), v((NX - 1, 8, C), F32),
            v((NZ, 16, C), BF16), v((NX, 8, C), F32), v((NY, 8, C), F32),
            v((NZ, 8, C), F32), v((NX, 8, C), F32),
            v((2, 1, C), F32), v((NX, 1, C), F32), v((NY, 1, C), F32), v((NZ, 1, C), F32),
            pltpu.SemaphoreType.REGULAR, dma((7,)), dma((2, 8)), dma((2, 8)), dma((70,)), dma((70,)), dma((110,)), dma((110,)),
        ],
        compiler_params=pltpu.CompilerParams(
            collective_id=0, has_side_effects=True, vmem_limit_bytes=60 * 1024 * 1024
        ),
        name="layer",
    )(
        fields, kernel.reshape(9 * C, C), bias.reshape(1, C), target,
        tile_list.reshape(8, 128), tail_count.reshape(1, NREG), region_weight.reshape(1, NREG),
    )
    results = (gf, gk, gb, rl)
    anywhere = pl.BlockSpec(memory_space=pl.ANY)
    gf, gk, gb, rl = pl.pallas_call(
        leave,
        out_shape=[jax.ShapeDtypeStruct(r.shape, r.dtype) for r in results],
        in_specs=[anywhere] * 4,
        out_specs=[anywhere] * 4,
        scratch_shapes=[pltpu.VMEM(r.shape, r.dtype) for r in results] + [dma((2, 7))],
        name="leave",
    )(*results)
    return gf, gk.reshape(3, 3, C, C), gb.reshape(C), rl.reshape(NREG)


def solution(mesh):
    placed = (P("lat", "lon", None), P(), P(), P("lat", "lon", None), P(), P(), P())
    return jax.shard_map(
        on_device,
        mesh=mesh,
        in_specs=placed,
        out_specs=(P("lat", "lon", None), P(), P(), P()),
        check_vma=False,
    )
```
